32 devices in a mesh: tm: 8 (over z, y), roi: 4 (over x, core).
Axes of the slice: x: 2, y: 2, z: 4, core: 2. Of those that a mesh axis runs over, the one named last changes fastest.
Arguments:
- movie: bfloat16 [128, 128, 2048], P('tm', None, 'roi'), may hold values from -6 to 6
- coeffs: bfloat16 [5, 128, 2048], P(None, 'tm', 'roi'), may hold values from -3 to 3
- footprint_w: bfloat16 [512, 3, 512], P(('tm', 'roi')), may hold values from -0.15625 to 0.15625
- roi_blocks: int32 [512, 3], P('tm'), may hold values from 0 to 63, as said below
- roi_len: int32 [512], P('tm'), may hold values from 1 to 3
Outputs:
- delta_field: bfloat16 [128, 128, 2048], P(None, 'tm', 'roi')
- traces: float32 [512, 128], P(('tm', 'roi'))
The draws below stay inside these ranges and needn't reach their ends.
Inputs may be any that keep to these rules, and one draw needn't show every extreme that they name: `roi_blocks`: entry m of ROI r names block slab * 16 + row: image row row of the group of r, inside column slab slab. The live entries of a ROI name distinct rows of one slab; entries past roi_len repeat the ROI's first entry. Over the 16 consecutive ROIs of one owner, the live entries from one slab name at most 3 distinct rows, and exactly 3 for some slab of every owner.
All inputs are finite; a program needn't handle non-finite values.
Results may differ from the reference program's by a relative error of at most 0.0049.
Values may be sent and summed in bfloat16 or wider, within the bound.
No kernel may reach another device: no remote copies, remote signals or barrier semaphores. Data moves between devices by JAX's collectives and lax.ppermute only.
A program may use at most 64 MiB of HBM per device.

```python
import jax
import jax.numpy as jnp
from jax import lax

COLS = 2048
ROW_DEV = 16
ROI_DEV = 16
TAPS = 5
BASE_WIN = 128
MAXB = 3
FRAMES = 128
ROWS = 128
BLK = 512
GROUP = 64
ROIS = 512
N_TM = 8
N_ROI = 4


def roi_layout(key):
    folded = jax.random.fold_in(key, 11)
    key_source, key_second, key_window, key_length, key_offset = jax.random.split(folded, 5)
    owners = GROUP // ROI_DEV
    group_count = ROIS // GROUP
    roi_index = jnp.arange(ROIS, dtype=jnp.int32)
    group_id = roi_index // GROUP
    owner_id = roi_index % GROUP // ROI_DEV
    leading = roi_index % ROI_DEV == 0
    spread = jnp.minimum(jax.random.randint(key_source, (ROIS,), 0, owners), jax.random.randint(key_second, (ROIS,), 0, owners))
    source = (owner_id + spread) % owners
    windows = jax.random.randint(key_window, (group_count, owners, owners), 0, ROW_DEV - MAXB + 1)
    length = jnp.where(leading, MAXB, jax.random.randint(key_length, (ROIS,), 1, MAXB + 1))
    offset = jax.random.randint(key_offset, (ROIS,), 0, MAXB) % (MAXB - length + 1)
    start_row = windows[group_id, owner_id, source] + offset
    column = jnp.arange(MAXB, dtype=jnp.int32)[None, :]
    row_ids = jnp.where(column < length[:, None], start_row[:, None] + column, start_row[:, None])
    return ((source[:, None] * ROW_DEV + row_ids).astype(jnp.int32), length.astype(jnp.int32))


def draw_roi_blocks(key, part):
    return roi_layout(key)[0]


def draw_roi_len(key, part):
    return roi_layout(key)[1]


def shard_levels(key, dims, cuts, smallest, largest):
    factor_of = 1.0
    for position, shards_of in cuts:
        heights = jax.random.uniform(jax.random.fold_in(jax.random.fold_in(key, 6), position), (shards_of,), jnp.float32, smallest / len(cuts), largest / len(cuts))
        factor_of = factor_of * jnp.repeat(jnp.exp(heights), dims[position] // shards_of).reshape((-1,) + (1,) * (len(dims) - 1 - position))
    return factor_of


def centred(own_key, dims, width, reach, cuts=(), kind=jnp.bfloat16):
    gain = shard_levels(own_key, dims, cuts, -0.22, 0.18) if cuts else 1.0
    entries = jax.random.normal(own_key, dims, jnp.float32) * width * gain
    return jnp.minimum(jnp.maximum(entries, -reach), reach).astype(kind)


def setup_inputs(seed: int = 0) -> dict:
    keys = jax.random.split(jax.random.key(seed), 6)
    return {
        "movie": centred(keys[0], (FRAMES, ROWS, COLS), 1.0, 6.0, ((0, 8), (2, 4))),
        "coeffs": centred(keys[1], (TAPS, ROWS, COLS), 0.5, 3.0, ((1, 8), (2, 4))),
        "footprint_w": centred(keys[2], (ROIS, MAXB, BLK), (MAXB * BLK) ** -0.5, 0.15625, ((0, 32),)),
        "roi_blocks": draw_roi_blocks(jax.random.fold_in(keys[5], 71), 0),
        "roi_len": draw_roi_len(jax.random.fold_in(keys[5], 71), 0),
    }


def reference(movie, coeffs, footprint_w, roi_blocks, roi_len):
    frame_ids = jnp.arange(FRAMES, dtype=jnp.int32)
    counts = jnp.minimum(frame_ids + 1, BASE_WIN).astype(jnp.float32)[:, None, None]
    slot_ids = jnp.arange(MAXB, dtype=jnp.int32)

    def per_group(group):
        row_start = (group * ROW_DEV).astype(jnp.int32)
        pixels = lax.dynamic_slice_in_dim(movie, row_start, ROW_DEV, 1).astype(jnp.float32)
        tap_weights = lax.dynamic_slice_in_dim(coeffs, row_start, ROW_DEV, 1).astype(jnp.float32)
        padded = jnp.pad(pixels, ((TAPS - 1, 0), (0, 0), (0, 0)))
        filtered = jnp.zeros(pixels.shape, jnp.float32)
        for delay_step in range(TAPS):
            lower = TAPS - 1 - delay_step
            filtered = filtered + tap_weights[delay_step] * padded[lower:lower + FRAMES]
        filtered = lax.optimization_barrier(filtered.astype(jnp.bfloat16)).astype(jnp.float32)
        running = jnp.cumsum(filtered, axis=0)
        earlier = jnp.pad(running, ((BASE_WIN, 0), (0, 0), (0, 0)))[:FRAMES]
        baseline = (running - earlier) / counts
        delta_field = (filtered - baseline).astype(jnp.bfloat16)
        first_roi = (group * GROUP).astype(jnp.int32)
        blocks = lax.dynamic_slice_in_dim(roi_blocks, first_roi, GROUP, 0)
        lengths = lax.dynamic_slice_in_dim(roi_len, first_roi, GROUP, 0)
        weights = lax.dynamic_slice_in_dim(footprint_w, first_roi, GROUP, 0).astype(jnp.float32)
        source = (blocks // ROW_DEV).astype(jnp.int32)
        local_row = (blocks % ROW_DEV).astype(jnp.int32)
        columns = delta_field.reshape(FRAMES, ROW_DEV, N_ROI, BLK)
        picked = columns[:, local_row, source, :].astype(jnp.float32)
        entry_used = (slot_ids[None, :] < lengths[:, None]).astype(jnp.float32)
        traces = jnp.einsum("tkmp,kmp->kt", picked, weights * entry_used[:, :, None])
        return delta_field, traces

    deltas, traces = lax.map(per_group, jnp.arange(N_TM, dtype=jnp.int32))
    delta_out = jnp.moveaxis(deltas, 0, 1).reshape(FRAMES, ROWS, COLS)
    return delta_out, traces.reshape(ROIS, FRAMES)
```

```python
import functools

import jax
import jax.numpy as jnp
from jax import lax
from jax.experimental import pallas as pl
from jax.experimental.pallas import tpu as pltpu
from jax.sharding import PartitionSpec as P

BASE_WIN = 128
LANES = 128


def chunk_kernel(
    ids_ref, inv_ref, coeff_ref, dense_ref, prev_ref, *rest, devices, owners
):
    blocks = rest[:devices]
    delta_ref = rest[devices]
    part_refs = rest[devices + 1 : devices + 1 + owners]
    pixels, filtered, delta32, partial = rest[devices + 1 + owners :]
    here = ids_ref[0]
    position = ids_ref[1]
    step, rows, width = blocks[0].shape
    taps = coeff_ref.shape[0]
    frames = devices * step
    for k in range(devices):
        start = pl.multiple_of((here ^ k) * step, step)
        pixels[pl.ds(start, step)] = blocks[k][...]

    for lane in range(0, width, LANES):
        span = slice(lane, lane + LANES)
        weights = [coeff_ref[k, :, span].astype(jnp.float32) for k in range(taps)]
        zero = jnp.zeros((rows, LANES), jnp.float32)

        def block_step(index, carry):
            running, history = carry[0], list(carry[1:])
            base = index * step
            for offset in range(step):
                frame = base + offset
                now = pixels[frame, :, span].astype(jnp.float32)
                total = weights[0] * now
                for k in range(1, taps):
                    total = total + weights[k] * history[k - 1]
                history = [now] + history[:-1]
                rounded = total.astype(jnp.bfloat16)
                value = rounded.astype(jnp.float32)
                running = running + value
                if frames > BASE_WIN:
                    filtered[frame, :, span] = rounded
                    gone = filtered[jnp.maximum(frame - BASE_WIN, 0), :, span]
                    running = running - jnp.where(
                        frame >= BASE_WIN, gone.astype(jnp.float32), 0.0
                    )
                delta = (value - running * inv_ref[frame]).astype(jnp.bfloat16)
                delta_ref[frame, :, span] = delta
                delta32[lane // LANES, pl.ds(frame * rows, rows), :] = delta.astype(
                    jnp.float32
                )
            return (running, *history)

        lax.fori_loop(0, devices, block_step, (zero,) * taps)

    total = prev_ref[...]
    for row in range(rows):
        picked = jnp.concatenate(
            [
                delta32[tile, pl.ds(row, frames, stride=rows), :].astype(jnp.bfloat16)
                for tile in range(width // LANES)
            ],
            axis=1,
        )
        total = total + lax.dot_general(
            dense_ref[row],
            picked,
            (((1,), (1,)), ((), ())),
            preferred_element_type=jnp.float32,
        )
    roi_here = total.shape[0] // owners
    partial[...] = total.reshape(owners, roi_here, frames)
    for k in range(owners):
        part_refs[k][...] = partial[position ^ k]


def run_chunk(ids, inverse, coeffs, dense, prev, blocks, owners):
    devices = len(blocks)
    step, rows, width = blocks[0].shape
    frames = devices * step
    rois = dense.shape[1]
    vmem = pl.BlockSpec(memory_space=pltpu.VMEM)
    smem = pl.BlockSpec(memory_space=pltpu.SMEM)
    held = frames if frames > BASE_WIN else 1
    return pl.pallas_call(
        functools.partial(chunk_kernel, devices=devices, owners=owners),
        out_shape=[jax.ShapeDtypeStruct((frames, rows, width), jnp.bfloat16)]
        + [jax.ShapeDtypeStruct((rois // owners, frames), jnp.float32)] * owners,
        in_specs=[smem, smem] + [vmem] * (3 + devices),
        out_specs=[vmem] * (1 + owners),
        scratch_shapes=[
            pltpu.VMEM((frames, rows, width), jnp.bfloat16),
            pltpu.VMEM((held, rows, width), jnp.bfloat16),
            pltpu.VMEM((width // LANES, frames * rows, LANES), jnp.float32),
            pltpu.VMEM((owners, rois // owners, frames), jnp.float32),
        ],
        compiler_params=pltpu.CompilerParams(vmem_limit_bytes=48 * 1024 * 1024),
        cost_estimate=pl.CostEstimate(
            flops=2 * frames * rows * width * rois,
            bytes_accessed=4 * frames * rows * width,
            transcendentals=0,
        ),
    )(ids, inverse, coeffs, dense, prev, *blocks)


def swaps(count, k):
    return [(i, i ^ k) for i in range(count)]


def local(movie, coeffs, footprint_w, roi_blocks, roi_len):
    devices = lax.axis_size("tm")
    owners = lax.axis_size("roi")
    here = lax.axis_index("tm")
    position = lax.axis_index("roi")
    step, _, slab_width = movie.shape
    rows = coeffs.shape[1]
    frames = devices * step
    slot_count = roi_blocks.shape[1]

    cuts = [0, slab_width - LANES, slab_width]
    order = list(range(devices - 1, 0, -1))
    chunks = []
    for low, high in zip(cuts[:-1], cuts[1:]):
        received = [None] * devices
        for k in order + [0]:
            block = lax.dynamic_slice(
                movie, (0, (here ^ k) * rows, low), (step, rows, high - low)
            )
            received[k] = lax.ppermute(block, "tm", swaps(devices, k)) if k else block
        chunks.append(received)

    gathered = lax.all_gather(footprint_w, "roi", axis=0, tiled=True)
    live = jnp.arange(slot_count, dtype=jnp.int32)[None, :] < roi_len[:, None]
    live = live & (roi_blocks // rows == position)
    hit = live[:, :, None] & (
        (roi_blocks % rows)[:, :, None] == jnp.arange(rows, dtype=jnp.int32)
    )
    dense = sum(
        jnp.where(hit[:, m, :].T[:, :, None], gathered[None, :, m, :], 0)
        for m in range(slot_count)
    ).astype(jnp.bfloat16)

    ids = jnp.stack([here, position]).astype(jnp.int32)
    counts = jnp.minimum(jnp.arange(frames, dtype=jnp.int32) + 1, BASE_WIN)
    inverse = 1.0 / counts.astype(jnp.float32)
    prev = jnp.zeros((dense.shape[1], frames), jnp.float32)
    deltas = []
    for low, high, received in zip(cuts[:-1], cuts[1:], chunks):
        delta, *parts = run_chunk(
            ids, inverse, coeffs[:, :, low:high], dense[:, :, low:high], prev, received, owners
        )
        deltas.append(delta)
        if high < slab_width:
            roi_here = parts[0].shape[0]
            stacked = jnp.stack(parts)
            back = jnp.arange(owners, dtype=jnp.int32) ^ position
            prev = stacked[back].reshape(owners * roi_here, frames)
    traces = parts[0]
    for k in range(1, owners):
        traces = traces + lax.ppermute(parts[k], "roi", swaps(owners, k))
    return jnp.concatenate(deltas, axis=2), traces


def solution(mesh):
    placed = (
        P("tm", None, "roi"),
        P(None, "tm", "roi"),
        P(("tm", "roi"), None, None),
        P("tm", None),
        P("tm"),
    )
    return jax.shard_map(
        local,
        mesh=mesh,
        in_specs=placed,
        out_specs=(P(None, "tm", "roi"), P(("tm", "roi"), None)),
        check_vma=False,
    )
```

```python
import functools

import jax
import jax.numpy as jnp
from jax import lax
from jax.experimental import pallas as pl
from jax.experimental.pallas import tpu as pltpu
from jax.sharding import PartitionSpec as P

BASE_WIN = 128
LANES = 128


def chunk_kernel(
    ids_ref, inv_ref, coeff_ref, dense_ref, prev_ref, *rest, places, owners
):
    devices = len(places)
    blocks = rest[:devices]
    delta_ref = rest[devices]
    part_refs = rest[devices + 1 : devices + 1 + owners]
    pixels, filtered, delta32, partial = rest[devices + 1 + owners :]
    here = ids_ref[0]
    position = ids_ref[1]
    _, rows, width = pixels.shape
    step = blocks[0].shape[0]
    taps = coeff_ref.shape[0]
    frames = devices * step
    for block, (k, offset) in zip(blocks, places):
        start = pl.multiple_of((here ^ k) * step, step)
        pixels[pl.ds(start, step)] = block[:, :, offset : offset + width]

    for lane in range(0, width, LANES):
        span = slice(lane, lane + LANES)
        weights = [coeff_ref[k, :, span].astype(jnp.float32) for k in range(taps)]
        zero = jnp.zeros((rows, LANES), jnp.float32)

        def block_step(index, carry):
            running, history = carry[0], list(carry[1:])
            base = index * step
            for offset in range(step):
                frame = base + offset
                now = pixels[frame, :, span].astype(jnp.float32)
                total = weights[0] * now
                for k in range(1, taps):
                    total = total + weights[k] * history[k - 1]
                history = [now] + history[:-1]
                rounded = total.astype(jnp.bfloat16)
                value = rounded.astype(jnp.float32)
                running = running + value
                if frames > BASE_WIN:
                    filtered[frame, :, span] = rounded
                    gone = filtered[jnp.maximum(frame - BASE_WIN, 0), :, span]
                    running = running - jnp.where(
                        frame >= BASE_WIN, gone.astype(jnp.float32), 0.0
                    )
                delta = (value - running * inv_ref[frame]).astype(jnp.bfloat16)
                delta_ref[frame, :, span] = delta
                delta32[lane // LANES, pl.ds(frame * rows, rows), :] = delta.astype(
                    jnp.float32
                )
            return (running, *history)

        lax.fori_loop(0, devices, block_step, (zero,) * taps)

    total = prev_ref[...]
    for row in range(rows):
        picked = jnp.concatenate(
            [
                delta32[tile, pl.ds(row, frames, stride=rows), :].astype(jnp.bfloat16)
                for tile in range(width // LANES)
            ],
            axis=1,
        )
        total = total + lax.dot_general(
            dense_ref[row],
            picked,
            (((1,), (1,)), ((), ())),
            preferred_element_type=jnp.float32,
        )
    roi_here = total.shape[0] // owners
    partial[...] = total.reshape(owners, roi_here, frames)
    for k in range(owners):
        part_refs[k][...] = partial[position ^ k]


def run_chunk(ids, inverse, coeffs, dense, prev, blocks, places, owners):
    devices = len(blocks)
    step = blocks[0].shape[0]
    _, rows, width = coeffs.shape
    frames = devices * step
    rois = dense.shape[1]
    vmem = pl.BlockSpec(memory_space=pltpu.VMEM)
    smem = pl.BlockSpec(memory_space=pltpu.SMEM)
    held = frames if frames > BASE_WIN else 1
    return pl.pallas_call(
        functools.partial(chunk_kernel, places=tuple(places), owners=owners),
        out_shape=[jax.ShapeDtypeStruct((frames, rows, width), jnp.bfloat16)]
        + [jax.ShapeDtypeStruct((rois // owners, frames), jnp.float32)] * owners,
        in_specs=[smem, smem] + [vmem] * (3 + devices),
        out_specs=[vmem] * (1 + owners),
        scratch_shapes=[
            pltpu.VMEM((frames, rows, width), jnp.bfloat16),
            pltpu.VMEM((held, rows, width), jnp.bfloat16),
            pltpu.VMEM((width // LANES, frames * rows, LANES), jnp.float32),
            pltpu.VMEM((owners, rois // owners, frames), jnp.float32),
        ],
        compiler_params=pltpu.CompilerParams(vmem_limit_bytes=24 * 1024 * 1024),
        cost_estimate=pl.CostEstimate(
            flops=2 * frames * rows * width * rois,
            bytes_accessed=4 * frames * rows * width,
            transcendentals=0,
        ),
    )(ids, inverse, coeffs, dense, prev, *blocks)


def swaps(count, k):
    return [(i, i ^ k) for i in range(count)]


def local(movie, coeffs, footprint_w, roi_blocks, roi_len):
    devices = lax.axis_size("tm")
    owners = lax.axis_size("roi")
    here = lax.axis_index("tm")
    position = lax.axis_index("roi")
    step, _, slab_width = movie.shape
    rows = coeffs.shape[1]
    frames = devices * step
    slot_count = roi_blocks.shape[1]

    middle = slab_width // LANES // 2 * LANES
    cuts = [0, middle, slab_width]
    near = list(range(devices // 2 - 1, 0, -1))
    far = list(range(devices - 1, devices // 2 - 1, -1))
    first = [(k, 0, middle) for k in far]
    whole = [(k, 0, slab_width) for k in near]
    second = [(k, middle, slab_width) for k in far]
    window = len(far) + 1
    sends, finish = first + whole[:1], []
    waiting, done = [], first[:-1] + whole[:1] + first[-1:] + whole[1:]
    for index, item in enumerate(second):
        waiting += [item] + whole[1 + index : 2 + index]
    sends += waiting
    finish = done[: len(waiting)]
    arrived = {}
    for turn, (k, low, high) in enumerate(sends):
        block = lax.dynamic_slice(
            movie, (0, (here ^ k) * rows, low), (step, rows, high - low)
        )
        if turn >= window and turn - window < len(finish):
            before = finish[turn - window]
            block, arrived[before] = lax.optimization_barrier((block, arrived[before]))
        arrived[k, low, high] = lax.ppermute(block, "tm", swaps(devices, k))
    arrived[0, 0, slab_width] = lax.dynamic_slice(
        movie, (0, here * rows, 0), (step, rows, slab_width)
    )
    chunks = []
    for low, high in zip(cuts[:-1], cuts[1:]):
        chunks.append(
            [
                (block, (k, low - start))
                for (k, start, end), block in arrived.items()
                if start <= low and high <= end
            ]
        )

    gathered = lax.all_gather(footprint_w, "roi", axis=0, tiled=True)
    live = jnp.arange(slot_count, dtype=jnp.int32)[None, :] < roi_len[:, None]
    live = live & (roi_blocks // rows == position)
    hit = live[:, :, None] & (
        (roi_blocks % rows)[:, :, None] == jnp.arange(rows, dtype=jnp.int32)
    )
    dense = sum(
        jnp.where(hit[:, m, :].T[:, :, None], gathered[None, :, m, :], 0)
        for m in range(slot_count)
    ).astype(jnp.bfloat16)

    ids = jnp.stack([here, position]).astype(jnp.int32)
    counts = jnp.minimum(jnp.arange(frames, dtype=jnp.int32) + 1, BASE_WIN)
    inverse = 1.0 / counts.astype(jnp.float32)
    prev = jnp.zeros((dense.shape[1], frames), jnp.float32)
    deltas = []
    for low, high, received in zip(cuts[:-1], cuts[1:], chunks):
        delta, *parts = run_chunk(
            ids,
            inverse,
            coeffs[:, :, low:high],
            dense[:, :, low:high],
            prev,
            [block for block, _ in received],
            [place for _, place in received],
            owners,
        )
        deltas.append(delta)
        if high < slab_width:
            roi_here = parts[0].shape[0]
            stacked = jnp.stack(parts)
            back = jnp.arange(owners, dtype=jnp.int32) ^ position
            prev = stacked[back].reshape(owners * roi_here, frames)
    traces = parts[0]
    for k in range(1, owners):
        traces = traces + lax.ppermute(parts[k], "roi", swaps(owners, k))
    return jnp.concatenate(deltas, axis=2), traces


def solution(mesh):
    placed = (
        P("tm", None, "roi"),
        P(None, "tm", "roi"),
        P(("tm", "roi"), None, None),
        P("tm", None),
        P("tm"),
    )
    return jax.shard_map(
        local,
        mesh=mesh,
        in_specs=placed,
        out_specs=(P(None, "tm", "roi"), P(("tm", "roi"), None)),
        check_vma=False,
    )
```

```python
import functools

import jax
import jax.numpy as jnp
from jax import lax
from jax.experimental import pallas as pl
from jax.experimental.pallas import tpu as pltpu
from jax.sharding import PartitionSpec as P

BASE_WIN = 128
LANES = 128


def chunk_kernel(
    ids_ref, inv_ref, coeff_ref, dense_ref, prev_ref, *rest, places, owners, last
):
    devices = len(places)
    parts = owners if last else 1
    blocks = rest[:devices]
    delta_ref = rest[devices]
    part_refs = rest[devices + 1 : devices + 1 + parts]
    pixels, filtered, delta32, partial = rest[devices + 1 + parts :]
    here = ids_ref[0]
    position = ids_ref[1]
    _, rows, width = pixels.shape
    step = blocks[0].shape[0]
    taps = coeff_ref.shape[0]
    frames = devices * step
    for block, (k, offset) in zip(blocks, places):
        start = pl.multiple_of((here ^ k) * step, step)
        pixels[pl.ds(start, step)] = block[:, :, offset : offset + width]

    for lane in range(0, width, LANES):
        span = slice(lane, lane + LANES)
        weights = [coeff_ref[k, :, span].astype(jnp.float32) for k in range(taps)]
        zero = jnp.zeros((rows, LANES), jnp.float32)

        def block_step(index, carry):
            running, history = carry[0], list(carry[1:])
            base = index * step
            for offset in range(step):
                frame = base + offset
                now = pixels[frame, :, span].astype(jnp.float32)
                total = weights[0] * now
                for k in range(1, taps):
                    total = total + weights[k] * history[k - 1]
                history = [now] + history[:-1]
                rounded = total.astype(jnp.bfloat16)
                value = rounded.astype(jnp.float32)
                running = running + value
                if frames > BASE_WIN:
                    filtered[frame, :, span] = rounded
                    gone = filtered[jnp.maximum(frame - BASE_WIN, 0), :, span]
                    running = running - jnp.where(
                        frame >= BASE_WIN, gone.astype(jnp.float32), 0.0
                    )
                delta = (value - running * inv_ref[frame]).astype(jnp.bfloat16)
                delta_ref[frame, :, span] = delta
                delta32[lane // LANES, pl.ds(frame * rows, rows), :] = delta.astype(
                    jnp.float32
                )
            return (running, *history)

        lax.fori_loop(0, devices, block_step, (zero,) * taps)

    total = prev_ref[...]
    for row in range(rows):
        picked = jnp.concatenate(
            [
                delta32[tile, pl.ds(row, frames, stride=rows), :].astype(jnp.bfloat16)
                for tile in range(width // LANES)
            ],
            axis=1,
        )
        total = total + lax.dot_general(
            dense_ref[row],
            picked,
            (((1,), (1,)), ((), ())),
            preferred_element_type=jnp.float32,
        )
    roi_here = total.shape[0] // owners
    if last:
        partial[...] = total.reshape(owners, roi_here, frames)
        for k in range(owners):
            part_refs[k][...] = partial[position ^ k]
    else:
        part_refs[0][...] = total


def run_chunk(ids, inverse, coeffs, dense, prev, blocks, places, owners, last):
    devices = len(blocks)
    step = blocks[0].shape[0]
    _, rows, width = coeffs.shape
    frames = devices * step
    rois = dense.shape[1]
    vmem = pl.BlockSpec(memory_space=pltpu.VMEM)
    smem = pl.BlockSpec(memory_space=pltpu.SMEM)
    held = frames if frames > BASE_WIN else 1
    parts = owners if last else 1
    return pl.pallas_call(
        functools.partial(chunk_kernel, places=tuple(places), owners=owners, last=last),
        out_shape=[jax.ShapeDtypeStruct((frames, rows, width), jnp.bfloat16)]
        + [jax.ShapeDtypeStruct((rois // parts, frames), jnp.float32)] * parts,
        in_specs=[smem, smem] + [vmem] * (3 + devices),
        out_specs=[vmem] * (1 + parts),
        scratch_shapes=[
            pltpu.VMEM((frames, rows, width), jnp.bfloat16),
            pltpu.VMEM((held, rows, width), jnp.bfloat16),
            pltpu.VMEM((width // LANES, frames * rows, LANES), jnp.float32),
            pltpu.VMEM((owners, rois // owners, frames), jnp.float32),
        ],
        compiler_params=pltpu.CompilerParams(vmem_limit_bytes=24 * 1024 * 1024),
        cost_estimate=pl.CostEstimate(
            flops=2 * frames * rows * width * rois,
            bytes_accessed=4 * frames * rows * width,
            transcendentals=0,
        ),
    )(ids, inverse, coeffs, dense, prev, *blocks)


def swaps(count, k):
    return [(i, i ^ k) for i in range(count)]


def local(movie, coeffs, footprint_w, roi_blocks, roi_len):
    devices = lax.axis_size("tm")
    owners = lax.axis_size("roi")
    here = lax.axis_index("tm")
    position = lax.axis_index("roi")
    step, _, slab_width = movie.shape
    rows = coeffs.shape[1]
    frames = devices * step
    slot_count = roi_blocks.shape[1]

    middle = slab_width // LANES // 2 * LANES
    cuts = [0, middle, slab_width]
    near = list(range(devices // 2 - 1, 0, -1))
    far = list(range(devices - 1, devices // 2 - 1, -1))
    split = far[len(far) // 2 :]
    opening = [(k, 0, slab_width) for k in far[: len(far) // 2]]
    beside = [(k, 0, slab_width) for k in near]
    first = [(k, 0, middle) for k in split]
    second = [(k, middle, slab_width) for k in split]
    ties = dict(zip(first + second, beside[::-1][: len(first) - 1] + opening + first))

    def rows_of(source, k, low, high):
        return lax.dynamic_slice(source, (0, (here ^ k) * rows, low), (step, rows, high - low))

    blocks = [rows_of(movie, *item) for item in opening]
    rest, *blocks = lax.optimization_barrier((movie, *blocks))
    arrived = {}
    for item in opening + beside + first + second:
        block = blocks.pop(0) if blocks else rows_of(rest, *item)
        if item in ties:
            block, arrived[ties[item]] = lax.optimization_barrier((block, arrived[ties[item]]))
        arrived[item] = lax.ppermute(block, "tm", swaps(devices, item[0]))
    arrived[0, 0, slab_width] = rows_of(rest, 0, 0, slab_width)
    chunks = []
    for low, high in zip(cuts[:-1], cuts[1:]):
        chunks.append(
            [
                (block, (k, low - start))
                for (k, start, end), block in arrived.items()
                if start <= low and high <= end
            ]
        )

    gathered = lax.all_gather(footprint_w, "roi", axis=0, tiled=True)
    live = jnp.arange(slot_count, dtype=jnp.int32)[None, :] < roi_len[:, None]
    live = live & (roi_blocks // rows == position)
    hit = live[:, :, None] & (
        (roi_blocks % rows)[:, :, None] == jnp.arange(rows, dtype=jnp.int32)
    )
    dense = sum(
        jnp.where(hit[:, m, :].T[:, :, None], gathered[None, :, m, :], 0)
        for m in range(slot_count)
    ).astype(jnp.bfloat16)

    ids = jnp.stack([here, position]).astype(jnp.int32)
    counts = jnp.minimum(jnp.arange(frames, dtype=jnp.int32) + 1, BASE_WIN)
    inverse = 1.0 / counts.astype(jnp.float32)
    prev = jnp.zeros((dense.shape[1], frames), jnp.float32)
    deltas = []
    for low, high, received in zip(cuts[:-1], cuts[1:], chunks):
        delta, *parts = run_chunk(
            ids,
            inverse,
            coeffs[:, :, low:high],
            dense[:, :, low:high],
            prev,
            [block for block, _ in received],
            [place for _, place in received],
            owners,
            high == slab_width,
        )
        deltas.append(delta)
        prev = parts[0]
    traces = parts[0]
    for k in range(1, owners):
        traces = traces + lax.ppermute(parts[k], "roi", swaps(owners, k))
    return jnp.concatenate(deltas, axis=2), traces


def solution(mesh):
    placed = (
        P("tm", None, "roi"),
        P(None, "tm", "roi"),
        P(("tm", "roi"), None, None),
        P("tm", None),
        P("tm"),
    )
    return jax.shard_map(
        local,
        mesh=mesh,
        in_specs=placed,
        out_specs=(P(None, "tm", "roi"), P(("tm", "roi"), None)),
        check_vma=False,
    )
```

```python
import functools

import jax
import jax.numpy as jnp
from jax import lax
from jax.experimental import pallas as pl
from jax.experimental.pallas import tpu as pltpu
from jax.sharding import PartitionSpec as P

BASE_WIN = 128
LANES = 128


def chunk_kernel(
    ids_ref, inv_ref, coeff_ref, dense_ref, prev_ref, *rest, places, owners, last
):
    devices = len(places)
    parts = owners if last else 1
    blocks = rest[:devices]
    delta_ref = rest[devices]
    part_refs = rest[devices + 1 : devices + 1 + parts]
    pixels, filtered, delta32, partial = rest[devices + 1 + parts :]
    here = ids_ref[0]
    position = ids_ref[1]
    _, rows, width = pixels.shape
    step = blocks[0].shape[0]
    taps = coeff_ref.shape[0]
    frames = devices * step
    for block, (k, offset) in zip(blocks, places):
        start = pl.multiple_of((here ^ k) * step, step)
        pixels[pl.ds(start, step)] = block[:, :, offset : offset + width]

    for lane in range(0, width, LANES):
        span = slice(lane, lane + LANES)
        weights = [coeff_ref[k, :, span].astype(jnp.float32) for k in range(taps)]
        zero = jnp.zeros((rows, LANES), jnp.float32)

        def block_step(index, carry):
            running, history = carry[0], list(carry[1:])
            base = index * step
            for offset in range(step):
                frame = base + offset
                now = pixels[frame, :, span].astype(jnp.float32)
                total = weights[0] * now
                for k in range(1, taps):
                    total = total + weights[k] * history[k - 1]
                history = [now] + history[:-1]
                rounded = total.astype(jnp.bfloat16)
                value = rounded.astype(jnp.float32)
                running = running + value
                if frames > BASE_WIN:
                    filtered[frame, :, span] = rounded
                    gone = filtered[jnp.maximum(frame - BASE_WIN, 0), :, span]
                    running = running - jnp.where(
                        frame >= BASE_WIN, gone.astype(jnp.float32), 0.0
                    )
                delta = (value - running * inv_ref[frame]).astype(jnp.bfloat16)
                delta_ref[frame, :, span] = delta
                delta32[lane // LANES, pl.ds(frame * rows, rows), :] = delta.astype(
                    jnp.float32
                )
            return (running, *history)

        lax.fori_loop(0, devices, block_step, (zero,) * taps)

    total = prev_ref[...]
    for row in range(rows):
        picked = jnp.concatenate(
            [
                delta32[tile, pl.ds(row, frames, stride=rows), :].astype(jnp.bfloat16)
                for tile in range(width // LANES)
            ],
            axis=1,
        )
        total = total + lax.dot_general(
            dense_ref[row],
            picked,
            (((1,), (1,)), ((), ())),
            preferred_element_type=jnp.float32,
        )
    roi_here = total.shape[0] // owners
    if last:
        partial[...] = total.reshape(owners, roi_here, frames)
        for k in range(owners):
            part_refs[k][...] = partial[position ^ k]
    else:
        part_refs[0][...] = total


def run_chunk(ids, inverse, coeffs, dense, prev, blocks, places, owners, last):
    devices = len(blocks)
    step = blocks[0].shape[0]
    _, rows, width = coeffs.shape
    frames = devices * step
    rois = dense.shape[1]
    vmem = pl.BlockSpec(memory_space=pltpu.VMEM)
    smem = pl.BlockSpec(memory_space=pltpu.SMEM)
    held = frames if frames > BASE_WIN else 1
    parts = owners if last else 1
    return pl.pallas_call(
        functools.partial(chunk_kernel, places=tuple(places), owners=owners, last=last),
        out_shape=[jax.ShapeDtypeStruct((frames, rows, width), jnp.bfloat16)]
        + [jax.ShapeDtypeStruct((rois // parts, frames), jnp.float32)] * parts,
        in_specs=[smem, smem] + [vmem] * (3 + devices),
        out_specs=[vmem] * (1 + parts),
        scratch_shapes=[
            pltpu.VMEM((frames, rows, width), jnp.bfloat16),
            pltpu.VMEM((held, rows, width), jnp.bfloat16),
            pltpu.VMEM((width // LANES, frames * rows, LANES), jnp.float32),
            pltpu.VMEM((owners, rois // owners, frames), jnp.float32),
        ],
        compiler_params=pltpu.CompilerParams(vmem_limit_bytes=24 * 1024 * 1024),
        cost_estimate=pl.CostEstimate(
            flops=2 * frames * rows * width * rois,
            bytes_accessed=4 * frames * rows * width,
            transcendentals=0,
        ),
    )(ids, inverse, coeffs, dense, prev, *blocks)


REACH = 8


def filtered_at(now, history, weights):
    total = weights[0] * now
    for tap in range(1, len(weights)):
        total = total + weights[tap] * history[tap - 1]
    return total.astype(jnp.bfloat16).astype(jnp.float32)


def tap_weights(coeff_ref, tile):
    span = slice(tile * LANES, (tile + 1) * LANES)
    return [coeff_ref[tap, :, span].astype(jnp.float32) for tap in range(coeff_ref.shape[0])]


def frame_rows(frame, rows):
    return pl.ds(pl.multiple_of(frame * rows, rows), rows)


def filter_rows(pixels, filtered, coeff_ref, frames, step):
    taps, rows, _ = coeff_ref.shape
    for tile in range(pixels.shape[0]):
        weights = tap_weights(coeff_ref, tile)

        def block_step(index, history):
            history = list(history)
            for offset in range(step):
                at = frame_rows(index * step + offset, rows)
                now = pixels[tile, at, :]
                filtered[tile, at, :] = filtered_at(now, history, weights)
                history = [now] + history[:-1]
            return tuple(history)

        zero = jnp.zeros((rows, LANES), jnp.float32)
        lax.fori_loop(0, frames // step, block_step, (zero,) * (taps - 1))


def subtract_mean(filtered, packed, inv_ref, step):
    tiles, frames, rows, _ = packed.shape

    def block_step(index, running):
        running = list(running)
        for offset in range(step):
            frame = index * step + offset
            for tile in range(tiles):
                value = filtered[tile, frame_rows(frame, rows), :]
                running[tile] = running[tile] + value
                packed[tile, frame] = (value - running[tile] * inv_ref[frame]).astype(
                    jnp.bfloat16
                )
        return tuple(running)

    zero = jnp.zeros((rows, LANES), jnp.float32)
    lax.fori_loop(0, frames // step, block_step, (zero,) * tiles)


def project(filtered, dense_ref, first, frames):
    rows = dense_ref.shape[0]
    total = 0.0
    for row in range(rows):
        picked = jnp.concatenate(
            [
                filtered[tile, pl.ds(first * rows + row, frames, stride=rows), :].astype(
                    jnp.bfloat16
                )
                for tile in range(filtered.shape[0])
            ],
            axis=1,
        )
        total = total + lax.dot_general(
            dense_ref[row],
            picked,
            (((1,), (1,)), ((), ())),
            preferred_element_type=jnp.float32,
        )
    return total


def send_out(packed, out_ref, first, sems):
    copies = [
        pltpu.make_async_copy(
            packed.at[tile], out_ref.at[:, :, pl.ds(first + tile * LANES, LANES)], sems.at[tile]
        )
        for tile in range(packed.shape[0])
    ]
    for copy in copies:
        copy.start()
    return copies


def fill(pixels, blocks, places, here, step, rows):
    for block, (k, lane) in zip(blocks, places):
        start = pl.multiple_of((here ^ k) * (step * rows), step * rows)
        for tile in range(pixels.shape[0]):
            first = lane + tile * LANES
            pixels[tile, pl.ds(start, step * rows), :] = block[
                :, first : first + LANES
            ].astype(jnp.float32)


def front_kernel(ids_ref, inv_ref, coeff_ref, dense_ref, *rest, places, step):
    blocks = rest[: len(places)]
    out_ref, total_ref, pixels, filtered, packed, sems = rest[len(places) :]
    frames, rows = inv_ref.shape[0], coeff_ref.shape[1]
    fill(pixels, blocks, places, ids_ref[0], step, rows)
    filter_rows(pixels, filtered, coeff_ref, frames, step)
    subtract_mean(filtered, packed, inv_ref, step)
    copies = send_out(packed, out_ref, 0, sems)
    total_ref[...] = project(filtered, dense_ref, 0, frames)
    for copy in copies:
        copy.wait()


def ready_kernel(ids_ref, coeff_ref, dense_ref, *rest, places, step, frames, late):
    blocks = rest[: len(places)]
    pixels, filtered, total_ref = rest[len(places) :]
    tiles, rows = pixels.shape[0], coeff_ref.shape[1]
    here = ids_ref[0]
    first = (here ^ late[-1]) // len(late) * (len(late) * step)
    span = (len(late) * step + REACH) * rows
    at = pl.ds(pl.multiple_of(first * rows, step * rows), span)
    for tile in range(tiles):
        pixels[tile, at, :] = jnp.zeros((span, LANES), jnp.float32)
    fill(pixels, blocks, places, here, step, rows)
    filter_rows(pixels, filtered, coeff_ref, frames, step)
    for tile in range(tiles):
        filtered[tile, at, :] = jnp.zeros((span, LANES), jnp.float32)
    total_ref[...] = project(filtered, dense_ref, 0, frames)


def trace_kernel(
    ids_ref, coeff_ref, dense_ref, front_ref, ready_ref, _px, _ft, *rest, late, owners
):
    blocks = rest[: len(late)]
    pixels, filtered, *part_refs = rest[len(late) : -2]
    strip, partial = rest[-2:]
    here, position = ids_ref[0], ids_ref[1]
    taps, rows, _ = coeff_ref.shape
    step = blocks[0].shape[0] // rows
    frames = front_ref.shape[1]
    first = (here ^ late[-1]) // len(late) * (len(late) * step)
    length = len(late) * step + REACH
    fill(pixels, blocks, [(k, 0) for k in late], here, step, rows)
    for tile in range(pixels.shape[0]):
        weights = tap_weights(coeff_ref, tile)
        history = []
        for tap in range(1, taps):
            earlier = pixels[tile, frame_rows(jnp.maximum(first - tap, 0), rows), :]
            history.append(jnp.where(first > 0, earlier, 0.0))

        def block_step(index, history):
            history = list(history)
            for offset in range(REACH):
                at = frame_rows(first + index * REACH + offset, rows)
                now = pixels[tile, at, :]
                filtered[tile, at, :] = filtered_at(now, history, weights)
                history = [now] + history[:-1]
            return tuple(history)

        lax.fori_loop(0, length // REACH, block_step, tuple(history))
    strip[...] = jnp.zeros(strip.shape, jnp.float32)
    strip[:, :length] = project(filtered, dense_ref, first, length)
    frame_ids = lax.broadcasted_iota(jnp.int32, strip.shape, 1)
    found = jnp.where(frame_ids < frames - first, strip[...], 0.0)
    total = front_ref[...] + ready_ref[...] + pltpu.roll(found, first, 1)
    running, reach = total, 1
    while reach < frames:
        shifted = pltpu.roll(running, reach, 1)
        running = running + jnp.where(frame_ids >= reach, shifted, 0.0)
        reach *= 2
    counts = jnp.minimum(frame_ids + 1, BASE_WIN).astype(jnp.float32)
    partial[...] = (total - running / counts).reshape(partial.shape)
    for k in range(owners):
        part_refs[k][...] = partial[position ^ k]


def delta_kernel(inv_ref, filtered, _, out_ref, packed, sems, *, first, step):
    subtract_mean(filtered, packed, inv_ref, step)
    for copy in send_out(packed, out_ref, first, sems):
        copy.wait()


VMEM = pl.BlockSpec(memory_space=pltpu.VMEM)
SMEM = pl.BlockSpec(memory_space=pltpu.SMEM)
ANYWHERE = pl.BlockSpec(memory_space=pl.ANY)


def options(mib, work):
    return dict(
        compiler_params=pltpu.CompilerParams(vmem_limit_bytes=mib * 1024 * 1024),
        cost_estimate=pl.CostEstimate(flops=16 * work, bytes_accessed=4 * work, transcendentals=0),
    )


def run_front(ids, inverse, coeffs, dense, blocks, places, slab_width):
    _, rows, width = coeffs.shape
    frames, tiles = inverse.shape[0], width // LANES
    step = blocks[0].shape[0] // rows
    held = pltpu.VMEM((tiles, frames * rows, LANES), jnp.float32)
    return pl.pallas_call(
        functools.partial(front_kernel, places=tuple(places), step=step),
        out_shape=[
            jax.ShapeDtypeStruct((frames, rows, slab_width), jnp.bfloat16),
            jax.ShapeDtypeStruct((dense.shape[1], frames), jnp.float32),
        ],
        in_specs=[SMEM, SMEM] + [VMEM] * (2 + len(blocks)),
        out_specs=[ANYWHERE, VMEM],
        scratch_shapes=[
            held,
            held,
            pltpu.VMEM((tiles, frames, rows, LANES), jnp.bfloat16),
            pltpu.SemaphoreType.DMA((tiles,)),
        ],
        **options(12, frames * rows * width),
    )(ids, inverse, coeffs, dense, *blocks)


def run_ready(ids, coeffs, dense, blocks, places, frames, late):
    _, rows, width = coeffs.shape
    step = blocks[0].shape[0] // rows
    held = jax.ShapeDtypeStruct((width // LANES, (frames + REACH) * rows, LANES), jnp.float32)
    return pl.pallas_call(
        functools.partial(
            ready_kernel, places=tuple(places), step=step, frames=frames, late=tuple(late)
        ),
        out_shape=[held, held, jax.ShapeDtypeStruct((dense.shape[1], frames), jnp.float32)],
        in_specs=[SMEM] + [VMEM] * (2 + len(blocks)),
        out_specs=[VMEM] * 3,
        **options(4, frames * rows * width),
    )(ids, coeffs, dense, *blocks)


def run_traces(ids, coeffs, dense, front, ready, pixels, filtered, late, owners):
    _, rows, width = coeffs.shape
    rois, frames = front.shape
    held = jax.ShapeDtypeStruct(pixels.shape, jnp.float32)
    part = jax.ShapeDtypeStruct((rois // owners, frames), jnp.float32)
    return pl.pallas_call(
        functools.partial(trace_kernel, late=tuple(late), owners=owners),
        out_shape=[held, held] + [part] * owners,
        in_specs=[SMEM] + [VMEM] * (6 + len(late)),
        out_specs=[VMEM] * (2 + owners),
        input_output_aliases={5: 0, 6: 1},
        scratch_shapes=[
            pltpu.VMEM((rois, frames), jnp.float32),
            pltpu.VMEM((owners, rois // owners, frames), jnp.float32),
        ],
        **options(4, frames * rows * width),
    )(ids, coeffs, dense, front, ready, pixels, filtered, *late.values())


def run_delta(inverse, filtered, out, first, rows, step):
    tiles, frames = filtered.shape[0], inverse.shape[0]
    return pl.pallas_call(
        functools.partial(delta_kernel, first=first, step=step),
        out_shape=jax.ShapeDtypeStruct(out.shape, jnp.bfloat16),
        in_specs=[SMEM, VMEM, ANYWHERE],
        out_specs=ANYWHERE,
        input_output_aliases={2: 0},
        scratch_shapes=[
            pltpu.VMEM((tiles, frames, rows, LANES), jnp.bfloat16),
            pltpu.SemaphoreType.DMA((tiles,)),
        ],
        **options(4, frames * rows * tiles * LANES),
    )(inverse, filtered, out)


def swaps(count, k):
    return [(i, i ^ k) for i in range(count)]


def plain_plan(movie, coeffs, dense_of, ids, inverse, here, position, devices, owners):
    step, _, slab_width = movie.shape
    rows = coeffs.shape[1]
    frames = devices * step
    middle = slab_width // LANES // 2 * LANES
    cuts = [0, middle, slab_width]
    near = list(range(devices // 2 - 1, 0, -1))
    far = list(range(devices - 1, devices // 2 - 1, -1))
    split = far[len(far) // 2 :]
    opening = [(k, 0, slab_width) for k in far[: len(far) // 2]]
    beside = [(k, 0, slab_width) for k in near]
    first = [(k, 0, middle) for k in split]
    second = [(k, middle, slab_width) for k in split]
    ties = dict(zip(first + second, beside[::-1][: len(first) - 1] + opening + first))

    def rows_of(source, k, low, high):
        return lax.dynamic_slice(source, (0, (here ^ k) * rows, low), (step, rows, high - low))

    blocks = [rows_of(movie, *item) for item in opening]
    rest, *blocks = lax.optimization_barrier((movie, *blocks))
    arrived = {}
    for item in opening + beside + first + second:
        block = blocks.pop(0) if blocks else rows_of(rest, *item)
        if item in ties:
            block, arrived[ties[item]] = lax.optimization_barrier((block, arrived[ties[item]]))
        arrived[item] = lax.ppermute(block, "tm", swaps(devices, item[0]))
    arrived[0, 0, slab_width] = rows_of(rest, 0, 0, slab_width)
    chunks = []
    for low, high in zip(cuts[:-1], cuts[1:]):
        chunks.append(
            [
                (block, (k, low - start))
                for (k, start, end), block in arrived.items()
                if start <= low and high <= end
            ]
        )

    dense = dense_of()
    prev = jnp.zeros((dense.shape[1], frames), jnp.float32)
    deltas = []
    for low, high, received in zip(cuts[:-1], cuts[1:], chunks):
        delta, *parts = run_chunk(
            ids,
            inverse,
            coeffs[:, :, low:high],
            dense[:, :, low:high],
            prev,
            [block for block, _ in received],
            [place for _, place in received],
            owners,
            high == slab_width,
        )
        deltas.append(delta)
        prev = parts[0]
    traces = parts[0]
    for k in range(1, owners):
        traces = traces + lax.ppermute(parts[k], "roi", swaps(owners, k))
    return jnp.concatenate(deltas, axis=2), traces


def local(movie, coeffs, footprint_w, roi_blocks, roi_len):
    devices = lax.axis_size("tm")
    owners = lax.axis_size("roi")
    here = lax.axis_index("tm")
    position = lax.axis_index("roi")
    step, _, slab_width = movie.shape
    rows = coeffs.shape[1]
    frames = devices * step
    slot_count = roi_blocks.shape[1]

    live = jnp.arange(slot_count, dtype=jnp.int32)[None, :] < roi_len[:, None]
    live = live & (roi_blocks // rows == position)
    hit = live[:, :, None] & (
        (roi_blocks % rows)[:, :, None] == jnp.arange(rows, dtype=jnp.int32)
    )

    def dense_of():
        gathered = lax.all_gather(footprint_w, "roi", axis=0, tiled=True)
        return sum(
            jnp.where(hit[:, m, :].T[:, :, None], gathered[None, :, m, :], 0)
            for m in range(slot_count)
        ).astype(jnp.bfloat16)

    counts = jnp.minimum(jnp.arange(frames, dtype=jnp.int32) + 1, BASE_WIN)
    inverse = 1.0 / counts.astype(jnp.float32)
    middle = slab_width // LANES // 2 * LANES
    ids = jnp.stack([here, position]).astype(jnp.int32)
    if frames > BASE_WIN or devices % 4 or middle == 0:
        return plain_plan(
            movie, coeffs, dense_of, ids, inverse, here, position, devices, owners
        )

    far = list(range(devices - 1, devices // 2 - 1, -1))
    near = list(range(devices // 2 - 1, 0, -1))
    early, late = far[: len(far) // 2], far[len(far) // 2 :]

    def rows_of(source, k, low=0, high=slab_width):
        block = lax.dynamic_slice(
            source, (0, (here ^ k) * rows, low), (step, rows, high - low)
        )
        return block.reshape(step * rows, high - low)

    def send(block, k, *after):
        if after:
            block, *_ = lax.optimization_barrier((block, *after))
        return lax.ppermute(block, "tm", swaps(devices, k))

    opening = [rows_of(movie, k) for k in early]
    rest, *opening = lax.optimization_barrier((movie, *opening))
    whole = {k: send(block, k) for block, k in zip(opening, early)}
    whole |= {k: send(rows_of(rest, k), k) for k in near}
    ties = [whole[near[-1]]] + [whole[k] for k in early]
    low = {k: send(rows_of(rest, k, 0, middle), k, tie) for k, tie in zip(late, ties)}
    ties = ties[len(late) :] + list(low.values())
    high = {k: send(rows_of(rest, k, middle), k, tie) for k, tie in zip(late, ties)}
    whole[0] = rows_of(rest, 0)
    dense = dense_of()

    blocks, places = list(whole.values()), list(whole)
    delta, front = run_front(
        ids,
        inverse,
        coeffs[:, :, :middle],
        dense[:, :, :middle],
        blocks + list(low.values()),
        [(k, 0) for k in places + late],
        slab_width,
    )
    second, heavy = coeffs[:, :, middle:], dense[:, :, middle:]
    pixels, filtered, ready = run_ready(
        ids, second, heavy, blocks, [(k, middle) for k in places], frames, late
    )
    _, filtered, *parts = run_traces(
        ids, second, heavy, front, ready, pixels, filtered, high, owners
    )
    traces = parts[0]
    for k in range(1, owners):
        traces = traces + lax.ppermute(parts[k], "roi", swaps(owners, k))
    return run_delta(inverse, filtered, delta, middle, rows, step), traces


def solution(mesh):
    placed = (
        P("tm", None, "roi"),
        P(None, "tm", "roi"),
        P(("tm", "roi"), None, None),
        P("tm", None),
        P("tm"),
    )
    return jax.shard_map(
        local,
        mesh=mesh,
        in_specs=placed,
        out_specs=(P(None, "tm", "roi"), P(("tm", "roi"), None)),
        check_vma=False,
    )
```

```python
import functools

import jax
import jax.numpy as jnp
from jax import lax
from jax.experimental import pallas as pl
from jax.experimental.pallas import tpu as pltpu
from jax.sharding import PartitionSpec as P

BASE_WIN = 128
LANES = 128


def chunk_kernel(
    ids_ref, inv_ref, coeff_ref, dense_ref, prev_ref, *rest, places, owners, last
):
    devices = len(places)
    parts = owners if last else 1
    blocks = rest[:devices]
    delta_ref = rest[devices]
    part_refs = rest[devices + 1 : devices + 1 + parts]
    pixels, filtered, delta32, partial = rest[devices + 1 + parts :]
    here = ids_ref[0]
    position = ids_ref[1]
    _, rows, width = pixels.shape
    step = blocks[0].shape[0]
    taps = coeff_ref.shape[0]
    frames = devices * step
    for block, (k, offset) in zip(blocks, places):
        start = pl.multiple_of((here ^ k) * step, step)
        pixels[pl.ds(start, step)] = block[:, :, offset : offset + width]

    for lane in range(0, width, LANES):
        span = slice(lane, lane + LANES)
        weights = [coeff_ref[k, :, span].astype(jnp.float32) for k in range(taps)]
        zero = jnp.zeros((rows, LANES), jnp.float32)

        def block_step(index, carry):
            running, history = carry[0], list(carry[1:])
            base = index * step
            for offset in range(step):
                frame = base + offset
                now = pixels[frame, :, span].astype(jnp.float32)
                total = weights[0] * now
                for k in range(1, taps):
                    total = total + weights[k] * history[k - 1]
                history = [now] + history[:-1]
                rounded = total.astype(jnp.bfloat16)
                value = rounded.astype(jnp.float32)
                running = running + value
                if frames > BASE_WIN:
                    filtered[frame, :, span] = rounded
                    gone = filtered[jnp.maximum(frame - BASE_WIN, 0), :, span]
                    running = running - jnp.where(
                        frame >= BASE_WIN, gone.astype(jnp.float32), 0.0
                    )
                delta = (value - running * inv_ref[frame]).astype(jnp.bfloat16)
                delta_ref[frame, :, span] = delta
                delta32[lane // LANES, pl.ds(frame * rows, rows), :] = delta.astype(
                    jnp.float32
                )
            return (running, *history)

        lax.fori_loop(0, devices, block_step, (zero,) * taps)

    total = prev_ref[...]
    for row in range(rows):
        picked = jnp.concatenate(
            [
                delta32[tile, pl.ds(row, frames, stride=rows), :].astype(jnp.bfloat16)
                for tile in range(width // LANES)
            ],
            axis=1,
        )
        total = total + lax.dot_general(
            dense_ref[row],
            picked,
            (((1,), (1,)), ((), ())),
            preferred_element_type=jnp.float32,
        )
    roi_here = total.shape[0] // owners
    if last:
        partial[...] = total.reshape(owners, roi_here, frames)
        for k in range(owners):
            part_refs[k][...] = partial[position ^ k]
    else:
        part_refs[0][...] = total


def run_chunk(ids, inverse, coeffs, dense, prev, blocks, places, owners, last):
    devices = len(blocks)
    step = blocks[0].shape[0]
    _, rows, width = coeffs.shape
    frames = devices * step
    rois = dense.shape[1]
    vmem = pl.BlockSpec(memory_space=pltpu.VMEM)
    smem = pl.BlockSpec(memory_space=pltpu.SMEM)
    held = frames if frames > BASE_WIN else 1
    parts = owners if last else 1
    return pl.pallas_call(
        functools.partial(chunk_kernel, places=tuple(places), owners=owners, last=last),
        out_shape=[jax.ShapeDtypeStruct((frames, rows, width), jnp.bfloat16)]
        + [jax.ShapeDtypeStruct((rois // parts, frames), jnp.float32)] * parts,
        in_specs=[smem, smem] + [vmem] * (3 + devices),
        out_specs=[vmem] * (1 + parts),
        scratch_shapes=[
            pltpu.VMEM((frames, rows, width), jnp.bfloat16),
            pltpu.VMEM((held, rows, width), jnp.bfloat16),
            pltpu.VMEM((width // LANES, frames * rows, LANES), jnp.float32),
            pltpu.VMEM((owners, rois // owners, frames), jnp.float32),
        ],
        compiler_params=pltpu.CompilerParams(vmem_limit_bytes=24 * 1024 * 1024),
        cost_estimate=pl.CostEstimate(
            flops=2 * frames * rows * width * rois,
            bytes_accessed=4 * frames * rows * width,
            transcendentals=0,
        ),
    )(ids, inverse, coeffs, dense, prev, *blocks)


REACH = 8


def filtered_at(now, history, weights):
    total = weights[0] * now
    for tap in range(1, len(weights)):
        total = total + weights[tap] * history[tap - 1]
    return total.astype(jnp.bfloat16).astype(jnp.float32)


def tap_weights(coeff_ref, tile):
    span = slice(tile * LANES, (tile + 1) * LANES)
    return [coeff_ref[tap, :, span].astype(jnp.float32) for tap in range(coeff_ref.shape[0])]


def frame_rows(frame, rows):
    return pl.ds(pl.multiple_of(frame * rows, rows), rows)


def filter_rows(pixels, filtered, coeff_ref, frames, step):
    taps, rows, _ = coeff_ref.shape
    for tile in range(pixels.shape[0]):
        weights = tap_weights(coeff_ref, tile)

        def block_step(index, history):
            history = list(history)
            for offset in range(step):
                at = frame_rows(index * step + offset, rows)
                now = pixels[tile, at, :]
                filtered[tile, at, :] = filtered_at(now, history, weights)
                history = [now] + history[:-1]
            return tuple(history)

        zero = jnp.zeros((rows, LANES), jnp.float32)
        lax.fori_loop(0, frames // step, block_step, (zero,) * (taps - 1))


def subtract_mean(filtered, packed, inv_ref, step):
    tiles, frames, rows, _ = packed.shape

    def block_step(index, running):
        running = list(running)
        for offset in range(step):
            frame = index * step + offset
            for tile in range(tiles):
                value = filtered[tile, frame_rows(frame, rows), :]
                running[tile] = running[tile] + value
                packed[tile, frame] = (value - running[tile] * inv_ref[frame]).astype(
                    jnp.bfloat16
                )
        return tuple(running)

    zero = jnp.zeros((rows, LANES), jnp.float32)
    lax.fori_loop(0, frames // step, block_step, (zero,) * tiles)


def project(filtered, dense_ref, first, frames):
    rows = dense_ref.shape[0]
    total = 0.0
    for row in range(rows):
        picked = jnp.concatenate(
            [
                filtered[tile, pl.ds(first * rows + row, frames, stride=rows), :].astype(
                    jnp.bfloat16
                )
                for tile in range(filtered.shape[0])
            ],
            axis=1,
        )
        total = total + lax.dot_general(
            dense_ref[row],
            picked,
            (((1,), (1,)), ((), ())),
            preferred_element_type=jnp.float32,
        )
    return total


def fill(pixels, blocks, places, here, step, rows):
    for block, (k, lane) in zip(blocks, places):
        start = pl.multiple_of((here ^ k) * (step * rows), step * rows)
        for tile in range(pixels.shape[0]):
            first = lane + tile * LANES
            pixels[tile, pl.ds(start, step * rows), :] = block[
                :, first : first + LANES
            ].astype(jnp.float32)


def late_frames(here, late, step):
    return (here ^ late[-1]) // len(late) * (len(late) * step), len(late) * step + REACH


def minus_mean(total):
    frames = total.shape[1]
    earlier = lax.broadcasted_iota(jnp.int32, (frames, frames), 0)
    later = lax.broadcasted_iota(jnp.int32, (frames, frames), 1)
    upto = jnp.where(earlier <= later, 1.0, 0.0).astype(jnp.bfloat16)
    high = total.astype(jnp.bfloat16)
    rest = total - high.astype(jnp.float32)
    middle = rest.astype(jnp.bfloat16)
    low = (rest - middle.astype(jnp.float32)).astype(jnp.bfloat16)
    running = sum(
        jnp.dot(term, upto, preferred_element_type=jnp.float32) for term in (low, middle, high)
    )
    frame_ids = lax.broadcasted_iota(jnp.int32, total.shape, 1)
    return total - running / jnp.minimum(frame_ids + 1, BASE_WIN).astype(jnp.float32)


def early_kernel(ids_ref, coeff_ref, dense_ref, *rest, places, step, frames, late):
    blocks = rest[: len(places)]
    pixels, filtered, total_ref = rest[len(places) :]
    rows = coeff_ref.shape[1]
    here = ids_ref[0]
    first, length = late_frames(here, late, step)
    at = pl.ds(pl.multiple_of(first * rows, step * rows), length * rows)
    zeros = jnp.zeros((length * rows, LANES), jnp.float32)
    for tile in range(pixels.shape[0]):
        pixels[tile, at, :] = zeros
    fill(pixels, blocks, [(k, 0) for k in places], here, step, rows)
    filter_rows(pixels, filtered, coeff_ref, frames, step)
    for tile in range(pixels.shape[0]):
        filtered[tile, at, :] = zeros
    total_ref[...] = project(filtered, dense_ref, 0, frames)


def late_kernel(ids_ref, coeff_ref, dense_ref, total_ref, _px, _ft, *rest, late, tile, last):
    blocks = rest[: len(late)]
    all_pixels, all_filtered, *outs, strip, partial = rest[len(late) :]
    here, position = ids_ref[0], ids_ref[1]
    taps, rows, width = coeff_ref.shape
    step = blocks[0].shape[0] // rows
    tiles = width // LANES
    frames = total_ref.shape[1]
    pixels = all_pixels.at[tile : tile + tiles]
    filtered = all_filtered.at[tile : tile + tiles]
    first, length = late_frames(here, late, step)
    fill(pixels, blocks, [(k, 0) for k in late], here, step, rows)
    for tile in range(tiles):
        weights = tap_weights(coeff_ref, tile)
        history = []
        for tap in range(1, taps):
            earlier = pixels[tile, frame_rows(jnp.maximum(first - tap, 0), rows), :]
            history.append(jnp.where(first > 0, earlier, 0.0))

        def block_step(index, history):
            history = list(history)
            for offset in range(REACH):
                at = frame_rows(first + index * REACH + offset, rows)
                now = pixels[tile, at, :]
                filtered[tile, at, :] = filtered_at(now, history, weights)
                history = [now] + history[:-1]
            return tuple(history)

        lax.fori_loop(0, length // REACH, block_step, tuple(history))
    strip[...] = jnp.zeros(strip.shape, jnp.float32)
    strip[:, :length] = project(filtered, dense_ref, first, length)
    frame_ids = lax.broadcasted_iota(jnp.int32, strip.shape, 1)
    found = jnp.where(frame_ids < frames - first, strip[...], 0.0)
    total = total_ref[...] + pltpu.roll(found, first, 1)
    if last:
        partial[...] = minus_mean(total).reshape(partial.shape)
        for k, out in enumerate(outs):
            out[...] = partial[position ^ k]
    else:
        outs[0][...] = total


def delta_kernel(inv_ref, filtered, out_ref, packed, sems, *, step):
    copies = []
    for tile in range(packed.shape[0]):
        at = pl.ds(tile, 1)
        subtract_mean(filtered.at[at], packed.at[at], inv_ref, step)
        place = out_ref.at[:, :, pl.ds(tile * LANES, LANES)]
        copies.append(pltpu.make_async_copy(packed.at[tile], place, sems.at[tile]))
        copies[-1].start()
    for copy in copies:
        copy.wait()


VMEM = pl.BlockSpec(memory_space=pltpu.VMEM)
SMEM = pl.BlockSpec(memory_space=pltpu.SMEM)
ANYWHERE = pl.BlockSpec(memory_space=pl.ANY)


def options(mib, work):
    return dict(
        compiler_params=pltpu.CompilerParams(vmem_limit_bytes=mib * 1024 * 1024),
        cost_estimate=pl.CostEstimate(flops=16 * work, bytes_accessed=4 * work, transcendentals=0),
    )


def run_early(ids, coeffs, dense, blocks, places, frames, late):
    _, rows, width = coeffs.shape
    step = blocks[0].shape[0] // rows
    held = jax.ShapeDtypeStruct((width // LANES, (frames + 2 * REACH) * rows, LANES), jnp.float32)
    return pl.pallas_call(
        functools.partial(
            early_kernel, places=tuple(places), step=step, frames=frames, late=tuple(late)
        ),
        out_shape=[held, held, jax.ShapeDtypeStruct((dense.shape[1], frames), jnp.float32)],
        in_specs=[SMEM] + [VMEM] * (2 + len(blocks)),
        out_specs=[VMEM] * 3,
        **options(4, frames * rows * width),
    )(ids, coeffs, dense, *blocks)


def run_late(ids, coeffs, dense, total, pixels, filtered, late, owners, tile, last):
    _, rows, width = coeffs.shape
    rois, frames = total.shape
    held = jax.ShapeDtypeStruct(pixels.shape, jnp.float32)
    parts = owners if last else 1
    part = jax.ShapeDtypeStruct((rois // parts, frames), jnp.float32)
    return pl.pallas_call(
        functools.partial(late_kernel, late=tuple(late), tile=tile, last=last),
        out_shape=[held, held] + [part] * parts,
        in_specs=[SMEM] + [VMEM] * (5 + len(late)),
        out_specs=[VMEM] * (2 + parts),
        input_output_aliases={4: 0, 5: 1},
        scratch_shapes=[
            pltpu.VMEM((rois, frames), jnp.float32),
            pltpu.VMEM((owners, rois // owners, frames), jnp.float32),
        ],
        **options(4, frames * rows * width),
    )(ids, coeffs, dense, total, pixels, filtered, *late.values())


def run_delta(inverse, filtered, rows, step):
    tiles, frames = filtered.shape[0], inverse.shape[0]
    return pl.pallas_call(
        functools.partial(delta_kernel, step=step),
        out_shape=jax.ShapeDtypeStruct((frames, rows, tiles * LANES), jnp.bfloat16),
        in_specs=[SMEM, VMEM],
        out_specs=ANYWHERE,
        scratch_shapes=[
            pltpu.VMEM((tiles, frames, rows, LANES), jnp.bfloat16),
            pltpu.SemaphoreType.DMA((tiles,)),
        ],
        **options(4, frames * rows * tiles * LANES),
    )(inverse, filtered)


def swaps(count, k):
    return [(i, i ^ k) for i in range(count)]


def plain_plan(movie, coeffs, dense_of, ids, inverse, here, position, devices, owners):
    step, _, slab_width = movie.shape
    rows = coeffs.shape[1]
    frames = devices * step
    middle = slab_width // LANES // 2 * LANES
    cuts = [0, middle, slab_width]
    near = list(range(devices // 2 - 1, 0, -1))
    far = list(range(devices - 1, devices // 2 - 1, -1))
    split = far[len(far) // 2 :]
    opening = [(k, 0, slab_width) for k in far[: len(far) // 2]]
    beside = [(k, 0, slab_width) for k in near]
    first = [(k, 0, middle) for k in split]
    second = [(k, middle, slab_width) for k in split]
    ties = dict(zip(first + second, beside[::-1][: len(first) - 1] + opening + first))

    def rows_of(source, k, low, high):
        return lax.dynamic_slice(source, (0, (here ^ k) * rows, low), (step, rows, high - low))

    blocks = [rows_of(movie, *item) for item in opening]
    rest, *blocks = lax.optimization_barrier((movie, *blocks))
    arrived = {}
    for item in opening + beside + first + second:
        block = blocks.pop(0) if blocks else rows_of(rest, *item)
        if item in ties:
            block, arrived[ties[item]] = lax.optimization_barrier((block, arrived[ties[item]]))
        arrived[item] = lax.ppermute(block, "tm", swaps(devices, item[0]))
    arrived[0, 0, slab_width] = rows_of(rest, 0, 0, slab_width)
    chunks = []
    for low, high in zip(cuts[:-1], cuts[1:]):
        chunks.append(
            [
                (block, (k, low - start))
                for (k, start, end), block in arrived.items()
                if start <= low and high <= end
            ]
        )

    dense = dense_of()
    prev = jnp.zeros((dense.shape[1], frames), jnp.float32)
    deltas = []
    for low, high, received in zip(cuts[:-1], cuts[1:], chunks):
        delta, *parts = run_chunk(
            ids,
            inverse,
            coeffs[:, :, low:high],
            dense[:, :, low:high],
            prev,
            [block for block, _ in received],
            [place for _, place in received],
            owners,
            high == slab_width,
        )
        deltas.append(delta)
        prev = parts[0]
    traces = parts[0]
    for k in range(1, owners):
        traces = traces + lax.ppermute(parts[k], "roi", swaps(owners, k))
    return jnp.concatenate(deltas, axis=2), traces


def local(movie, coeffs, footprint_w, roi_blocks, roi_len):
    devices = lax.axis_size("tm")
    owners = lax.axis_size("roi")
    here = lax.axis_index("tm")
    position = lax.axis_index("roi")
    step, _, slab_width = movie.shape
    rows = coeffs.shape[1]
    frames = devices * step
    slot_count = roi_blocks.shape[1]

    live = jnp.arange(slot_count, dtype=jnp.int32)[None, :] < roi_len[:, None]
    live = live & (roi_blocks // rows == position)
    hit = live[:, :, None] & (
        (roi_blocks % rows)[:, :, None] == jnp.arange(rows, dtype=jnp.int32)
    )

    def dense_of():
        gathered = lax.all_gather(footprint_w, "roi", axis=0, tiled=True)
        return sum(
            jnp.where(hit[:, m, :].T[:, :, None], gathered[None, :, m, :], 0)
            for m in range(slot_count)
        ).astype(jnp.bfloat16)

    counts = jnp.minimum(jnp.arange(frames, dtype=jnp.int32) + 1, BASE_WIN)
    inverse = 1.0 / counts.astype(jnp.float32)
    middle = slab_width - LANES
    ids = jnp.stack([here, position]).astype(jnp.int32)
    if frames > BASE_WIN or devices % 4 or middle == 0:
        return plain_plan(
            movie, coeffs, dense_of, ids, inverse, here, position, devices, owners
        )

    far = list(range(devices - 1, devices // 2 - 1, -1))
    near = list(range(devices // 2 - 1, 0, -1))
    early, late = far[: len(far) // 2], far[len(far) // 2 :]

    def rows_of(source, k, low=0, high=slab_width):
        block = lax.dynamic_slice(
            source, (0, (here ^ k) * rows, low), (step, rows, high - low)
        )
        return block.reshape(step * rows, high - low)

    def send(block, k, *after):
        if after:
            block, *_ = lax.optimization_barrier((block, *after))
        return lax.ppermute(block, "tm", swaps(devices, k))

    opening = [rows_of(movie, k) for k in early]
    rest, *opening = lax.optimization_barrier((movie, *opening))
    whole = {k: send(block, k) for block, k in zip(opening, early)}
    whole |= {k: send(rows_of(rest, k), k) for k in near}
    ties = [whole[near[-1]]] + [whole[k] for k in early]
    low = {k: send(rows_of(rest, k, 0, middle), k, tie) for k, tie in zip(late, ties)}
    ties = ties[len(late) :] + list(low.values())
    high = {k: send(rows_of(rest, k, middle), k, tie) for k, tie in zip(late, ties)}
    whole[0] = rows_of(rest, 0)
    dense = dense_of()

    pixels, filtered, total = run_early(
        ids, coeffs, dense, list(whole.values()), list(whole), frames, late
    )
    pixels, filtered, total = run_late(
        ids,
        coeffs[:, :, :middle],
        dense[:, :, :middle],
        total,
        pixels,
        filtered,
        low,
        owners,
        0,
        False,
    )
    _, filtered, *parts = run_late(
        ids,
        coeffs[:, :, middle:],
        dense[:, :, middle:],
        total,
        pixels,
        filtered,
        high,
        owners,
        middle // LANES,
        True,
    )
    traces = parts[0]
    for k in range(owners - 1, 0, -1):
        traces = traces + lax.ppermute(parts[k], "roi", swaps(owners, k))
    return run_delta(inverse, filtered, rows, step), traces


def solution(mesh):
    placed = (
        P("tm", None, "roi"),
        P(None, "tm", "roi"),
        P(("tm", "roi"), None, None),
        P("tm", None),
        P("tm"),
    )
    return jax.shard_map(
        local,
        mesh=mesh,
        in_specs=placed,
        out_specs=(P(None, "tm", "roi"), P(("tm", "roi"), None)),
        check_vma=False,
    )
```

```python
import functools

import jax
import jax.numpy as jnp
from jax import lax
from jax.experimental import pallas as pl
from jax.experimental.pallas import tpu as pltpu
from jax.sharding import PartitionSpec as P

BASE_WIN = 128
LANES = 128


def chunk_kernel(
    ids_ref, inv_ref, coeff_ref, dense_ref, prev_ref, *rest, places, owners, last
):
    devices = len(places)
    parts = owners if last else 1
    blocks = rest[:devices]
    delta_ref = rest[devices]
    part_refs = rest[devices + 1 : devices + 1 + parts]
    pixels, filtered, delta32, partial = rest[devices + 1 + parts :]
    here = ids_ref[0]
    position = ids_ref[1]
    _, rows, width = pixels.shape
    step = blocks[0].shape[0]
    taps = coeff_ref.shape[0]
    frames = devices * step
    for block, (k, offset) in zip(blocks, places):
        start = pl.multiple_of((here ^ k) * step, step)
        pixels[pl.ds(start, step)] = block[:, :, offset : offset + width]

    for lane in range(0, width, LANES):
        span = slice(lane, lane + LANES)
        weights = [coeff_ref[k, :, span].astype(jnp.float32) for k in range(taps)]
        zero = jnp.zeros((rows, LANES), jnp.float32)

        def block_step(index, carry):
            running, history = carry[0], list(carry[1:])
            base = index * step
            for offset in range(step):
                frame = base + offset
                now = pixels[frame, :, span].astype(jnp.float32)
                total = weights[0] * now
                for k in range(1, taps):
                    total = total + weights[k] * history[k - 1]
                history = [now] + history[:-1]
                rounded = total.astype(jnp.bfloat16)
                value = rounded.astype(jnp.float32)
                running = running + value
                if frames > BASE_WIN:
                    filtered[frame, :, span] = rounded
                    gone = filtered[jnp.maximum(frame - BASE_WIN, 0), :, span]
                    running = running - jnp.where(
                        frame >= BASE_WIN, gone.astype(jnp.float32), 0.0
                    )
                delta = (value - running * inv_ref[frame]).astype(jnp.bfloat16)
                delta_ref[frame, :, span] = delta
                delta32[lane // LANES, pl.ds(frame * rows, rows), :] = delta.astype(
                    jnp.float32
                )
            return (running, *history)

        lax.fori_loop(0, devices, block_step, (zero,) * taps)

    total = prev_ref[...]
    for row in range(rows):
        picked = jnp.concatenate(
            [
                delta32[tile, pl.ds(row, frames, stride=rows), :].astype(jnp.bfloat16)
                for tile in range(width // LANES)
            ],
            axis=1,
        )
        total = total + lax.dot_general(
            dense_ref[row],
            picked,
            (((1,), (1,)), ((), ())),
            preferred_element_type=jnp.float32,
        )
    roi_here = total.shape[0] // owners
    if last:
        partial[...] = total.reshape(owners, roi_here, frames)
        for k in range(owners):
            part_refs[k][...] = partial[position ^ k]
    else:
        part_refs[0][...] = total


def run_chunk(ids, inverse, coeffs, dense, prev, blocks, places, owners, last):
    devices = len(blocks)
    step = blocks[0].shape[0]
    _, rows, width = coeffs.shape
    frames = devices * step
    rois = dense.shape[1]
    vmem = pl.BlockSpec(memory_space=pltpu.VMEM)
    smem = pl.BlockSpec(memory_space=pltpu.SMEM)
    held = frames if frames > BASE_WIN else 1
    parts = owners if last else 1
    return pl.pallas_call(
        functools.partial(chunk_kernel, places=tuple(places), owners=owners, last=last),
        out_shape=[jax.ShapeDtypeStruct((frames, rows, width), jnp.bfloat16)]
        + [jax.ShapeDtypeStruct((rois // parts, frames), jnp.float32)] * parts,
        in_specs=[smem, smem] + [vmem] * (3 + devices),
        out_specs=[vmem] * (1 + parts),
        scratch_shapes=[
            pltpu.VMEM((frames, rows, width), jnp.bfloat16),
            pltpu.VMEM((held, rows, width), jnp.bfloat16),
            pltpu.VMEM((width // LANES, frames * rows, LANES), jnp.float32),
            pltpu.VMEM((owners, rois // owners, frames), jnp.float32),
        ],
        compiler_params=pltpu.CompilerParams(vmem_limit_bytes=24 * 1024 * 1024),
        cost_estimate=pl.CostEstimate(
            flops=2 * frames * rows * width * rois,
            bytes_accessed=4 * frames * rows * width,
            transcendentals=0,
        ),
    )(ids, inverse, coeffs, dense, prev, *blocks)


REACH = 8


def filtered_at(now, history, weights):
    total = weights[0] * now
    for tap in range(1, len(weights)):
        total = total + weights[tap] * history[tap - 1]
    return total.astype(jnp.bfloat16).astype(jnp.float32)


def tap_weights(coeff_ref, tile):
    span = slice(tile * LANES, (tile + 1) * LANES)
    return [coeff_ref[tap, :, span].astype(jnp.float32) for tap in range(coeff_ref.shape[0])]


def frame_rows(frame, rows):
    return pl.ds(pl.multiple_of(frame * rows, rows), rows)


def filter_rows(pixels, filtered, coeff_ref, frames, step):
    taps, rows, _ = coeff_ref.shape
    for tile in range(pixels.shape[0]):
        weights = tap_weights(coeff_ref, tile)

        def block_step(index, history):
            history = list(history)
            for offset in range(step):
                at = frame_rows(index * step + offset, rows)
                now = pixels[tile, at, :]
                filtered[tile, at, :] = filtered_at(now, history, weights)
                history = [now] + history[:-1]
            return tuple(history)

        zero = jnp.zeros((rows, LANES), jnp.float32)
        lax.fori_loop(0, frames // step, block_step, (zero,) * (taps - 1))


def project(filtered, dense_ref, first, frames):
    rows = dense_ref.shape[0]
    total = 0.0
    for row in range(rows):
        picked = jnp.concatenate(
            [
                filtered[tile, pl.ds(first * rows + row, frames, stride=rows), :].astype(
                    jnp.bfloat16
                )
                for tile in range(filtered.shape[0])
            ],
            axis=1,
        )
        total = total + lax.dot_general(
            dense_ref[row],
            picked,
            (((1,), (1,)), ((), ())),
            preferred_element_type=jnp.float32,
        )
    return total


def fill(pixels, blocks, places, here, step, rows):
    for block, (k, lane) in zip(blocks, places):
        start = pl.multiple_of((here ^ k) * (step * rows), step * rows)
        for tile in range(pixels.shape[0]):
            first = lane + tile * LANES
            pixels[tile, pl.ds(start, step * rows), :] = block[
                :, first : first + LANES
            ].astype(jnp.float32)


def late_frames(here, late, step):
    return (here ^ late[-1]) // len(late) * (len(late) * step), len(late) * step + REACH


def minus_mean(total):
    frames = total.shape[1]
    earlier = lax.broadcasted_iota(jnp.int32, (frames, frames), 0)
    later = lax.broadcasted_iota(jnp.int32, (frames, frames), 1)
    upto = jnp.where(earlier <= later, 1.0, 0.0).astype(jnp.bfloat16)
    high = total.astype(jnp.bfloat16)
    rest = total - high.astype(jnp.float32)
    middle = rest.astype(jnp.bfloat16)
    low = (rest - middle.astype(jnp.float32)).astype(jnp.bfloat16)
    running = sum(
        jnp.dot(term, upto, preferred_element_type=jnp.float32) for term in (low, middle, high)
    )
    frame_ids = lax.broadcasted_iota(jnp.int32, total.shape, 1)
    return total - running / jnp.minimum(frame_ids + 1, BASE_WIN).astype(jnp.float32)


def early_kernel(ids_ref, coeff_ref, dense_ref, *rest, places, step, frames, late):
    blocks = rest[: len(places)]
    pixels, filtered, total_ref = rest[len(places) :]
    rows = coeff_ref.shape[1]
    here = ids_ref[0]
    first, length = late_frames(here, late, step)
    at = pl.ds(pl.multiple_of(first * rows, step * rows), length * rows)
    zeros = jnp.zeros((length * rows, LANES), jnp.float32)
    for tile in range(pixels.shape[0]):
        pixels[tile, at, :] = zeros
    fill(pixels, blocks, [(k, 0) for k in places], here, step, rows)
    filter_rows(pixels, filtered, coeff_ref, frames, step)
    for tile in range(pixels.shape[0]):
        filtered[tile, at, :] = zeros
    total_ref[...] = project(filtered, dense_ref, 0, frames)


def late_kernel(ids_ref, coeff_ref, dense_ref, total_ref, pixels, *rest, late, first_tile, last):
    blocks = rest[: len(late)]
    filtered, *outs, held, strip, partial = rest[len(late) :]
    here, position = ids_ref[0], ids_ref[1]
    taps, rows, width = coeff_ref.shape
    step = blocks[0].shape[0] // rows
    frames = total_ref.shape[1]
    first, length = late_frames(here, late, step)
    for tile in range(width // LANES):
        own = pixels.at[first_tile + tile]
        for block, k in zip(blocks, late):
            start = pl.multiple_of(((here ^ k) * step - first) * rows, step * rows)
            held[pl.ds(start, step * rows), :] = block[
                :, tile * LANES : (tile + 1) * LANES
            ].astype(jnp.float32)
        after = pl.multiple_of((first + length - REACH) * rows, step * rows)
        held[(length - REACH) * rows :, :] = own[pl.ds(after, REACH * rows), :]
        weights = tap_weights(coeff_ref, tile)
        history = []
        for tap in range(1, taps):
            earlier = own[frame_rows(jnp.maximum(first - tap, 0), rows), :]
            history.append(jnp.where(first > 0, earlier, 0.0))

        def block_step(index, history):
            history = list(history)
            for offset in range(REACH):
                at = frame_rows(index * REACH + offset, rows)
                now = held[at, :]
                filtered[tile, at, :] = filtered_at(now, history, weights)
                history = [now] + history[:-1]
            return tuple(history)

        lax.fori_loop(0, length // REACH, block_step, tuple(history))
    strip[...] = jnp.zeros(strip.shape, jnp.float32)
    strip[:, :length] = project(filtered, dense_ref, 0, length)
    frame_ids = lax.broadcasted_iota(jnp.int32, strip.shape, 1)
    found = jnp.where(frame_ids < frames - first, strip[...], 0.0)
    total = total_ref[...] + pltpu.roll(found, first, 1)
    if last:
        partial[...] = minus_mean(total).reshape(partial.shape)
        for k, out in enumerate(outs):
            out[...] = partial[position ^ k]
    else:
        outs[0][...] = total


def delta_kernel(ids_ref, inv_ref, *rest, late, step):
    *pieces, filtered, out_ref, packed, sems = rest
    pieces = pieces[::-1]
    tiles, frames, rows, _ = packed.shape
    first, length = late_frames(ids_ref[0], late, step)
    places = [(piece, tile) for piece in pieces for tile in range(piece.shape[0])]
    copies = []
    for tile, (piece, its_tile) in enumerate(places):

        def subtract_mean(source, low, high, running):
            def block_step(index, running):
                for offset in range(REACH):
                    frame = index * REACH + offset
                    value = source(frame)
                    running = running + value
                    packed[tile, frame] = (value - running * inv_ref[frame]).astype(jnp.bfloat16)
                return running

            return lax.fori_loop(low // REACH, high // REACH, block_step, running)

        def early(frame):
            return filtered[tile, frame_rows(frame, rows), :]

        def middle(frame):
            return piece[its_tile, frame_rows(frame - first, rows), :]

        end = jnp.minimum(first + length, frames)
        running = subtract_mean(early, 0, first, jnp.zeros((rows, LANES), jnp.float32))
        running = subtract_mean(middle, first, end, running)
        subtract_mean(early, end, frames, running)
        place = out_ref.at[:, :, pl.ds(tile * LANES, LANES)]
        copies.append(pltpu.make_async_copy(packed.at[tile], place, sems.at[tile]))
        copies[-1].start()
    for copy in copies:
        copy.wait()


VMEM = pl.BlockSpec(memory_space=pltpu.VMEM)
SMEM = pl.BlockSpec(memory_space=pltpu.SMEM)
ANYWHERE = pl.BlockSpec(memory_space=pl.ANY)


def options(mib, work):
    return dict(
        compiler_params=pltpu.CompilerParams(vmem_limit_bytes=mib * 1024 * 1024),
        cost_estimate=pl.CostEstimate(flops=16 * work, bytes_accessed=4 * work, transcendentals=0),
    )


def run_early(ids, coeffs, dense, blocks, places, frames, late):
    _, rows, width = coeffs.shape
    step = blocks[0].shape[0] // rows
    held = jax.ShapeDtypeStruct((width // LANES, (frames + 2 * REACH) * rows, LANES), jnp.float32)
    return pl.pallas_call(
        functools.partial(
            early_kernel, places=tuple(places), step=step, frames=frames, late=tuple(late)
        ),
        out_shape=[held, held, jax.ShapeDtypeStruct((dense.shape[1], frames), jnp.float32)],
        in_specs=[SMEM] + [VMEM] * (2 + len(blocks)),
        out_specs=[VMEM] * 3,
        **options(4, frames * rows * width),
    )(ids, coeffs, dense, *blocks)


def run_late(ids, coeffs, dense, total, pixels, late, owners, first_tile, last):
    _, rows, width = coeffs.shape
    rois, frames = total.shape
    height = sum(block.shape[0] for block in late.values()) + REACH * rows
    parts = owners if last else 1
    part = jax.ShapeDtypeStruct((rois // parts, frames), jnp.float32)
    return pl.pallas_call(
        functools.partial(late_kernel, late=tuple(late), first_tile=first_tile, last=last),
        out_shape=[jax.ShapeDtypeStruct((width // LANES, height, LANES), jnp.float32)]
        + [part] * parts,
        in_specs=[SMEM] + [VMEM] * (4 + len(late)),
        out_specs=[VMEM] * (1 + parts),
        scratch_shapes=[
            pltpu.VMEM((height, LANES), jnp.float32),
            pltpu.VMEM((rois, frames), jnp.float32),
            pltpu.VMEM((owners, rois // owners, frames), jnp.float32),
        ],
        **options(4, frames * rows * width),
    )(ids, coeffs, dense, total, pixels, *late.values())


def run_delta(ids, inverse, filtered, pieces, late, rows, step):
    tiles, frames = filtered.shape[0], inverse.shape[0]
    return pl.pallas_call(
        functools.partial(delta_kernel, late=tuple(late), step=step),
        out_shape=jax.ShapeDtypeStruct((frames, rows, tiles * LANES), jnp.bfloat16),
        in_specs=[SMEM, SMEM] + [VMEM] * (1 + len(pieces)),
        out_specs=ANYWHERE,
        scratch_shapes=[
            pltpu.VMEM((tiles, frames, rows, LANES), jnp.bfloat16),
            pltpu.SemaphoreType.DMA((tiles,)),
        ],
        **options(4, frames * rows * tiles * LANES),
    )(ids, inverse, *pieces[::-1], filtered)


def swaps(count, k):
    return [(i, i ^ k) for i in range(count)]


def plain_plan(movie, coeffs, dense_of, ids, inverse, here, position, devices, owners):
    step, _, slab_width = movie.shape
    rows = coeffs.shape[1]
    frames = devices * step
    middle = slab_width // LANES // 2 * LANES
    cuts = [0, middle, slab_width]
    near = list(range(devices // 2 - 1, 0, -1))
    far = list(range(devices - 1, devices // 2 - 1, -1))
    split = far[len(far) // 2 :]
    opening = [(k, 0, slab_width) for k in far[: len(far) // 2]]
    beside = [(k, 0, slab_width) for k in near]
    first = [(k, 0, middle) for k in split]
    second = [(k, middle, slab_width) for k in split]
    ties = dict(zip(first + second, beside[::-1][: len(first) - 1] + opening + first))

    def rows_of(source, k, low, high):
        return lax.dynamic_slice(source, (0, (here ^ k) * rows, low), (step, rows, high - low))

    blocks = [rows_of(movie, *item) for item in opening]
    rest, *blocks = lax.optimization_barrier((movie, *blocks))
    arrived = {}
    for item in opening + beside + first + second:
        block = blocks.pop(0) if blocks else rows_of(rest, *item)
        if item in ties:
            block, arrived[ties[item]] = lax.optimization_barrier((block, arrived[ties[item]]))
        arrived[item] = lax.ppermute(block, "tm", swaps(devices, item[0]))
    arrived[0, 0, slab_width] = rows_of(rest, 0, 0, slab_width)
    chunks = []
    for low, high in zip(cuts[:-1], cuts[1:]):
        chunks.append(
            [
                (block, (k, low - start))
                for (k, start, end), block in arrived.items()
                if start <= low and high <= end
            ]
        )

    dense = dense_of()
    prev = jnp.zeros((dense.shape[1], frames), jnp.float32)
    deltas = []
    for low, high, received in zip(cuts[:-1], cuts[1:], chunks):
        delta, *parts = run_chunk(
            ids,
            inverse,
            coeffs[:, :, low:high],
            dense[:, :, low:high],
            prev,
            [block for block, _ in received],
            [place for _, place in received],
            owners,
            high == slab_width,
        )
        deltas.append(delta)
        prev = parts[0]
    traces = parts[0]
    for k in range(1, owners):
        traces = traces + lax.ppermute(parts[k], "roi", swaps(owners, k))
    return jnp.concatenate(deltas, axis=2), traces


def local(movie, coeffs, footprint_w, roi_blocks, roi_len):
    devices = lax.axis_size("tm")
    owners = lax.axis_size("roi")
    here = lax.axis_index("tm")
    position = lax.axis_index("roi")
    step, _, slab_width = movie.shape
    rows = coeffs.shape[1]
    frames = devices * step
    slot_count = roi_blocks.shape[1]

    live = jnp.arange(slot_count, dtype=jnp.int32)[None, :] < roi_len[:, None]
    live = live & (roi_blocks // rows == position)
    hit = live[:, :, None] & (
        (roi_blocks % rows)[:, :, None] == jnp.arange(rows, dtype=jnp.int32)
    )

    def dense_of():
        gathered = lax.all_gather(footprint_w, "roi", axis=0, tiled=True)
        return sum(
            jnp.where(hit[:, m, :].T[:, :, None], gathered[None, :, m, :], 0)
            for m in range(slot_count)
        ).astype(jnp.bfloat16)

    counts = jnp.minimum(jnp.arange(frames, dtype=jnp.int32) + 1, BASE_WIN)
    inverse = 1.0 / counts.astype(jnp.float32)
    middle = slab_width - LANES
    ids = jnp.stack([here, position]).astype(jnp.int32)
    if frames > BASE_WIN or devices % 4 or middle == 0:
        return plain_plan(
            movie, coeffs, dense_of, ids, inverse, here, position, devices, owners
        )

    far = list(range(devices - 1, devices // 2 - 1, -1))
    near = list(range(1, devices // 2))
    early, late = far[: len(far) // 2], far[len(far) // 2 :]

    def rows_of(source, k, low=0, high=slab_width):
        block = lax.dynamic_slice(
            source, (0, (here ^ k) * rows, low), (step, rows, high - low)
        )
        return block.reshape(step * rows, high - low)

    def send(block, k, *after):
        if after:
            block, *_ = lax.optimization_barrier((block, *after))
        return lax.ppermute(block, "tm", swaps(devices, k))

    opening = [rows_of(movie, k) for k in early]
    rest, *opening = lax.optimization_barrier((movie, *opening))
    whole = {k: send(block, k) for block, k in zip(opening, early)}
    whole |= {k: send(rows_of(rest, k), k) for k in near}
    ties = [whole[near[0]]] + [whole[k] for k in early]
    low = {k: send(rows_of(rest, k, 0, middle), k, tie) for k, tie in zip(late, ties)}
    ties = ties[len(late) :] + list(low.values())
    high = {k: send(rows_of(rest, k, middle), k, tie) for k, tie in zip(late, ties)}
    whole[0] = rows_of(rest, 0)
    dense = dense_of()

    pixels, filtered, total = run_early(
        ids, coeffs, dense, list(whole.values()), list(whole), frames, late
    )
    lower, total = run_late(
        ids,
        coeffs[:, :, :middle],
        dense[:, :, :middle],
        total,
        pixels,
        low,
        owners,
        0,
        False,
    )
    pixels, filtered, lower, total = lax.optimization_barrier(
        (pixels, filtered, lower, total)
    )
    upper, *parts = run_late(
        ids,
        coeffs[:, :, middle:],
        dense[:, :, middle:],
        total,
        pixels,
        high,
        owners,
        middle // LANES,
        True,
    )
    traces = parts[0]
    for k in range(1, owners):
        traces = traces + lax.ppermute(parts[k], "roi", swaps(owners, k))
    delta = run_delta(ids, inverse, filtered, [lower, upper], late, rows, step)
    return delta, traces


def solution(mesh):
    placed = (
        P("tm", None, "roi"),
        P(None, "tm", "roi"),
        P(("tm", "roi"), None, None),
        P("tm", None),
        P("tm"),
    )
    return jax.shard_map(
        local,
        mesh=mesh,
        in_specs=placed,
        out_specs=(P(None, "tm", "roi"), P(("tm", "roi"), None)),
        check_vma=False,
    )
```

```python
import functools

import jax
import jax.numpy as jnp
from jax import lax
from jax.experimental import pallas as pl
from jax.experimental.pallas import tpu as pltpu
from jax.sharding import PartitionSpec as P

BASE_WIN = 128
LANES = 128


def chunk_kernel(
    ids_ref, inv_ref, coeff_ref, dense_ref, prev_ref, *rest, places, owners, last
):
    devices = len(places)
    parts = owners if last else 1
    blocks = rest[:devices]
    delta_ref = rest[devices]
    part_refs = rest[devices + 1 : devices + 1 + parts]
    pixels, filtered, delta32, partial = rest[devices + 1 + parts :]
    here = ids_ref[0]
    position = ids_ref[1]
    _, rows, width = pixels.shape
    step = blocks[0].shape[0]
    taps = coeff_ref.shape[0]
    frames = devices * step
    for block, (k, offset) in zip(blocks, places):
        start = pl.multiple_of((here ^ k) * step, step)
        pixels[pl.ds(start, step)] = block[:, :, offset : offset + width]

    for lane in range(0, width, LANES):
        span = slice(lane, lane + LANES)
        weights = [coeff_ref[k, :, span].astype(jnp.float32) for k in range(taps)]
        zero = jnp.zeros((rows, LANES), jnp.float32)

        def block_step(index, carry):
            running, history = carry[0], list(carry[1:])
            base = index * step
            for offset in range(step):
                frame = base + offset
                now = pixels[frame, :, span].astype(jnp.float32)
                total = weights[0] * now
                for k in range(1, taps):
                    total = total + weights[k] * history[k - 1]
                history = [now] + history[:-1]
                rounded = total.astype(jnp.bfloat16)
                value = rounded.astype(jnp.float32)
                running = running + value
                if frames > BASE_WIN:
                    filtered[frame, :, span] = rounded
                    gone = filtered[jnp.maximum(frame - BASE_WIN, 0), :, span]
                    running = running - jnp.where(
                        frame >= BASE_WIN, gone.astype(jnp.float32), 0.0
                    )
                delta = (value - running * inv_ref[frame]).astype(jnp.bfloat16)
                delta_ref[frame, :, span] = delta
                delta32[lane // LANES, pl.ds(frame * rows, rows), :] = delta.astype(
                    jnp.float32
                )
            return (running, *history)

        lax.fori_loop(0, devices, block_step, (zero,) * taps)

    total = prev_ref[...]
    for row in range(rows):
        picked = jnp.concatenate(
            [
                delta32[tile, pl.ds(row, frames, stride=rows), :].astype(jnp.bfloat16)
                for tile in range(width // LANES)
            ],
            axis=1,
        )
        total = total + lax.dot_general(
            dense_ref[row],
            picked,
            (((1,), (1,)), ((), ())),
            preferred_element_type=jnp.float32,
        )
    roi_here = total.shape[0] // owners
    if last:
        partial[...] = total.reshape(owners, roi_here, frames)
        for k in range(owners):
            part_refs[k][...] = partial[position ^ k]
    else:
        part_refs[0][...] = total


def run_chunk(ids, inverse, coeffs, dense, prev, blocks, places, owners, last):
    devices = len(blocks)
    step = blocks[0].shape[0]
    _, rows, width = coeffs.shape
    frames = devices * step
    rois = dense.shape[1]
    vmem = pl.BlockSpec(memory_space=pltpu.VMEM)
    smem = pl.BlockSpec(memory_space=pltpu.SMEM)
    held = frames if frames > BASE_WIN else 1
    parts = owners if last else 1
    return pl.pallas_call(
        functools.partial(chunk_kernel, places=tuple(places), owners=owners, last=last),
        out_shape=[jax.ShapeDtypeStruct((frames, rows, width), jnp.bfloat16)]
        + [jax.ShapeDtypeStruct((rois // parts, frames), jnp.float32)] * parts,
        in_specs=[smem, smem] + [vmem] * (3 + devices),
        out_specs=[vmem] * (1 + parts),
        scratch_shapes=[
            pltpu.VMEM((frames, rows, width), jnp.bfloat16),
            pltpu.VMEM((held, rows, width), jnp.bfloat16),
            pltpu.VMEM((width // LANES, frames * rows, LANES), jnp.float32),
            pltpu.VMEM((owners, rois // owners, frames), jnp.float32),
        ],
        compiler_params=pltpu.CompilerParams(vmem_limit_bytes=24 * 1024 * 1024),
        cost_estimate=pl.CostEstimate(
            flops=2 * frames * rows * width * rois,
            bytes_accessed=4 * frames * rows * width,
            transcendentals=0,
        ),
    )(ids, inverse, coeffs, dense, prev, *blocks)


REACH = 8


def filtered_at(now, history, weights):
    total = weights[0] * now
    for tap in range(1, len(weights)):
        total = total + weights[tap] * history[tap - 1]
    return total.astype(jnp.bfloat16).astype(jnp.float32)


def tap_weights(coeff_ref, tile):
    span = slice(tile * LANES, (tile + 1) * LANES)
    return [coeff_ref[tap, :, span].astype(jnp.float32) for tap in range(coeff_ref.shape[0])]


def frame_rows(frame, rows):
    return pl.ds(pl.multiple_of(frame * rows, rows), rows)


def filter_rows(pixels, filtered, coeff_ref, frames, step):
    taps, rows, _ = coeff_ref.shape
    for tile in range(pixels.shape[0]):
        weights = tap_weights(coeff_ref, tile)

        def block_step(index, history):
            history = list(history)
            for offset in range(step):
                at = frame_rows(index * step + offset, rows)
                now = pixels[tile, at, :]
                filtered[tile, at, :] = filtered_at(now, history, weights)
                history = [now] + history[:-1]
            return tuple(history)

        zero = jnp.zeros((rows, LANES), jnp.float32)
        lax.fori_loop(0, frames // step, block_step, (zero,) * (taps - 1))


def project(filtered, dense_ref, first, frames):
    rows = dense_ref.shape[0]
    total = 0.0
    for row in range(rows):
        picked = jnp.concatenate(
            [
                filtered[tile, pl.ds(first * rows + row, frames, stride=rows), :].astype(
                    jnp.bfloat16
                )
                for tile in range(filtered.shape[0])
            ],
            axis=1,
        )
        total = total + lax.dot_general(
            dense_ref[row],
            picked,
            (((1,), (1,)), ((), ())),
            preferred_element_type=jnp.float32,
        )
    return total


def fill(pixels, blocks, places, here, step, rows):
    for block, (k, lane) in zip(blocks, places):
        start = pl.multiple_of((here ^ k) * (step * rows), step * rows)
        for tile in range(pixels.shape[0]):
            first = lane + tile * LANES
            pixels[tile, pl.ds(start, step * rows), :] = block[
                :, first : first + LANES
            ].astype(jnp.float32)


def late_frames(here, late, step):
    return (here ^ late[-1]) // len(late) * (len(late) * step), len(late) * step + REACH


def minus_mean(total):
    frames = total.shape[1]
    earlier = lax.broadcasted_iota(jnp.int32, (frames, frames), 0)
    later = lax.broadcasted_iota(jnp.int32, (frames, frames), 1)
    upto = jnp.where(earlier <= later, 1.0, 0.0).astype(jnp.bfloat16)
    high = total.astype(jnp.bfloat16)
    rest = total - high.astype(jnp.float32)
    middle = rest.astype(jnp.bfloat16)
    low = (rest - middle.astype(jnp.float32)).astype(jnp.bfloat16)
    running = sum(
        jnp.dot(term, upto, preferred_element_type=jnp.float32) for term in (low, middle, high)
    )
    frame_ids = lax.broadcasted_iota(jnp.int32, total.shape, 1)
    return total - running / jnp.minimum(frame_ids + 1, BASE_WIN).astype(jnp.float32)


def early_kernel(coeff_ref, dense_ref, *rest, places, step, frames, late):
    blocks = rest[: len(places)]
    pixels, filtered, total_ref = rest[len(places) :]
    rows = coeff_ref.shape[1]
    here = lax.axis_index("tm")
    first, length = late_frames(here, late, step)
    at = pl.ds(pl.multiple_of(first * rows, step * rows), length * rows)
    zeros = jnp.zeros((length * rows, LANES), jnp.float32)
    for tile in range(pixels.shape[0]):
        pixels[tile, at, :] = zeros
    fill(pixels, blocks, [(k, 0) for k in places], here, step, rows)
    filter_rows(pixels, filtered, coeff_ref, frames, step)
    for tile in range(pixels.shape[0]):
        filtered[tile, at, :] = zeros
    total_ref[...] = project(filtered, dense_ref, 0, frames)


def late_kernel(coeff_ref, dense_ref, total_ref, pixels, *rest, late, first_tile, last):
    blocks = rest[: len(late)]
    filtered, *outs, held, strip, partial = rest[len(late) :]
    here, position = lax.axis_index("tm"), lax.axis_index("roi")
    taps, rows, width = coeff_ref.shape
    step = blocks[0].shape[0] // rows
    frames = total_ref.shape[1]
    first, length = late_frames(here, late, step)
    for tile in range(width // LANES):
        own = pixels.at[first_tile + tile]
        for block, k in zip(blocks, late):
            start = pl.multiple_of(((here ^ k) * step - first) * rows, step * rows)
            held[pl.ds(start, step * rows), :] = block[
                :, tile * LANES : (tile + 1) * LANES
            ].astype(jnp.float32)
        after = pl.multiple_of((first + length - REACH) * rows, step * rows)
        held[(length - REACH) * rows :, :] = own[pl.ds(after, REACH * rows), :]
        weights = tap_weights(coeff_ref, tile)
        history = []
        for tap in range(1, taps):
            earlier = own[frame_rows(jnp.maximum(first - tap, 0), rows), :]
            history.append(jnp.where(first > 0, earlier, 0.0))

        def block_step(index, history):
            history = list(history)
            for offset in range(REACH):
                at = frame_rows(index * REACH + offset, rows)
                now = held[at, :]
                filtered[tile, at, :] = filtered_at(now, history, weights)
                history = [now] + history[:-1]
            return tuple(history)

        lax.fori_loop(0, length // REACH, block_step, tuple(history))
    strip[...] = jnp.zeros(strip.shape, jnp.float32)
    strip[:, :length] = project(filtered, dense_ref, 0, length)
    frame_ids = lax.broadcasted_iota(jnp.int32, strip.shape, 1)
    found = jnp.where(frame_ids < frames - first, strip[...], 0.0)
    total = total_ref[...] + pltpu.roll(found, first, 1)
    if last:
        partial[...] = minus_mean(total).reshape(partial.shape)
        for k, out in enumerate(outs):
            out[...] = partial[position ^ k]
    else:
        outs[0][...] = total


def delta_kernel(*rest, late, step):
    *pieces, filtered, out_ref, inv_ref, packed, sems = rest
    tiles, frames, rows, _ = packed.shape
    first, length = late_frames(lax.axis_index("tm"), late, step)
    end = jnp.minimum(first + length, frames)
    counts = lax.broadcasted_iota(jnp.int32, (frames, LANES), 0) + 1
    inv_ref[...] = 1.0 / jnp.minimum(counts, BASE_WIN).astype(jnp.float32)
    places = [(piece, tile) for piece in pieces[::-1] for tile in range(piece.shape[0])]
    copies = []
    for tile in range(0, tiles, 2):
        several = range(tile, min(tile + 2, tiles))

        def subtract_mean(source, low, high, running):
            def block_step(index, running):
                running = list(running)
                for offset in range(REACH):
                    frame = index * REACH + offset
                    for turn, one in enumerate(several):
                        value = source(one, frame)
                        running[turn] = running[turn] + value
                        packed[one, frame] = (value - running[turn] * inv_ref[pl.ds(frame, 1), :]).astype(
                            jnp.bfloat16
                        )
                return tuple(running)

            return lax.fori_loop(low // REACH, high // REACH, block_step, running)

        def early(one, frame):
            return filtered[one, frame_rows(frame, rows), :]

        def middle(one, frame):
            piece, its_tile = places[one]
            return piece[its_tile, frame_rows(frame - first, rows), :]

        zero = jnp.zeros((rows, LANES), jnp.float32)
        running = subtract_mean(early, 0, first, (zero,) * len(several))
        running = subtract_mean(middle, first, end, running)
        subtract_mean(early, end, frames, running)
        for one in several:
            place = out_ref.at[:, :, pl.ds(one * LANES, LANES)]
            copies.append(pltpu.make_async_copy(packed.at[one], place, sems.at[one]))
            copies[-1].start()
    for copy in copies:
        copy.wait()


VMEM = pl.BlockSpec(memory_space=pltpu.VMEM)
SMEM = pl.BlockSpec(memory_space=pltpu.SMEM)
ANYWHERE = pl.BlockSpec(memory_space=pl.ANY)


def options(mib, work):
    return dict(
        compiler_params=pltpu.CompilerParams(vmem_limit_bytes=mib * 1024 * 1024),
        cost_estimate=pl.CostEstimate(flops=16 * work, bytes_accessed=4 * work, transcendentals=0),
    )


def run_early(coeffs, dense, blocks, places, frames, late):
    _, rows, width = coeffs.shape
    step = blocks[0].shape[0] // rows
    held = jax.ShapeDtypeStruct((width // LANES, (frames + 2 * REACH) * rows, LANES), jnp.float32)
    return pl.pallas_call(
        functools.partial(
            early_kernel, places=tuple(places), step=step, frames=frames, late=tuple(late)
        ),
        out_shape=[held, held, jax.ShapeDtypeStruct((dense.shape[1], frames), jnp.float32)],
        in_specs=[VMEM] * (2 + len(blocks)),
        out_specs=[VMEM] * 3,
        **options(4, frames * rows * width),
    )(coeffs, dense, *blocks)


def run_late(coeffs, dense, total, pixels, late, owners, first_tile, last):
    _, rows, width = coeffs.shape
    rois, frames = total.shape
    height = sum(block.shape[0] for block in late.values()) + REACH * rows
    parts = owners if last else 1
    part = jax.ShapeDtypeStruct((rois // parts, frames), jnp.float32)
    return pl.pallas_call(
        functools.partial(late_kernel, late=tuple(late), first_tile=first_tile, last=last),
        out_shape=[jax.ShapeDtypeStruct((width // LANES, height, LANES), jnp.float32)]
        + [part] * parts,
        in_specs=[VMEM] * (4 + len(late)),
        out_specs=[VMEM] * (1 + parts),
        scratch_shapes=[
            pltpu.VMEM((height, LANES), jnp.float32),
            pltpu.VMEM((rois, frames), jnp.float32),
            pltpu.VMEM((owners, rois // owners, frames), jnp.float32),
        ],
        **options(4, frames * rows * width),
    )(coeffs, dense, total, pixels, *late.values())


def run_delta(filtered, pieces, late, rows, step):
    tiles, frames = filtered.shape[0], filtered.shape[1] // rows - 2 * REACH
    return pl.pallas_call(
        functools.partial(delta_kernel, late=tuple(late), step=step),
        out_shape=jax.ShapeDtypeStruct((frames, rows, tiles * LANES), jnp.bfloat16),
        in_specs=[VMEM] * (1 + len(pieces)),
        out_specs=ANYWHERE,
        scratch_shapes=[
            pltpu.VMEM((frames, LANES), jnp.float32),
            pltpu.VMEM((tiles, frames, rows, LANES), jnp.bfloat16),
            pltpu.SemaphoreType.DMA((tiles,)),
        ],
        **options(4, frames * rows * tiles * LANES),
    )(*pieces[::-1], filtered)


def swaps(count, k):
    return [(i, i ^ k) for i in range(count)]


def plain_plan(movie, coeffs, dense_of, ids, inverse, here, position, devices, owners):
    step, _, slab_width = movie.shape
    rows = coeffs.shape[1]
    frames = devices * step
    middle = slab_width // LANES // 2 * LANES
    cuts = [0, middle, slab_width]
    near = list(range(devices // 2 - 1, 0, -1))
    far = list(range(devices - 1, devices // 2 - 1, -1))
    split = far[len(far) // 2 :]
    opening = [(k, 0, slab_width) for k in far[: len(far) // 2]]
    beside = [(k, 0, slab_width) for k in near]
    first = [(k, 0, middle) for k in split]
    second = [(k, middle, slab_width) for k in split]
    ties = dict(zip(first + second, beside[::-1][: len(first) - 1] + opening + first))

    def rows_of(source, k, low, high):
        return lax.dynamic_slice(source, (0, (here ^ k) * rows, low), (step, rows, high - low))

    blocks = [rows_of(movie, *item) for item in opening]
    rest, *blocks = lax.optimization_barrier((movie, *blocks))
    arrived = {}
    for item in opening + beside + first + second:
        block = blocks.pop(0) if blocks else rows_of(rest, *item)
        if item in ties:
            block, arrived[ties[item]] = lax.optimization_barrier((block, arrived[ties[item]]))
        arrived[item] = lax.ppermute(block, "tm", swaps(devices, item[0]))
    arrived[0, 0, slab_width] = rows_of(rest, 0, 0, slab_width)
    chunks = []
    for low, high in zip(cuts[:-1], cuts[1:]):
        chunks.append(
            [
                (block, (k, low - start))
                for (k, start, end), block in arrived.items()
                if start <= low and high <= end
            ]
        )

    dense = dense_of()
    prev = jnp.zeros((dense.shape[1], frames), jnp.float32)
    deltas = []
    for low, high, received in zip(cuts[:-1], cuts[1:], chunks):
        delta, *parts = run_chunk(
            ids,
            inverse,
            coeffs[:, :, low:high],
            dense[:, :, low:high],
            prev,
            [block for block, _ in received],
            [place for _, place in received],
            owners,
            high == slab_width,
        )
        deltas.append(delta)
        prev = parts[0]
    traces = parts[0]
    for k in range(1, owners):
        traces = traces + lax.ppermute(parts[k], "roi", swaps(owners, k))
    return jnp.concatenate(deltas, axis=2), traces


def local(movie, coeffs, footprint_w, roi_blocks, roi_len):
    devices = lax.axis_size("tm")
    owners = lax.axis_size("roi")
    here = lax.axis_index("tm")
    position = lax.axis_index("roi")
    step, _, slab_width = movie.shape
    rows = coeffs.shape[1]
    frames = devices * step
    slot_count = roi_blocks.shape[1]

    live = jnp.arange(slot_count, dtype=jnp.int32)[None, :] < roi_len[:, None]
    live = live & (roi_blocks // rows == position)
    hit = live[:, :, None] & (
        (roi_blocks % rows)[:, :, None] == jnp.arange(rows, dtype=jnp.int32)
    )

    def dense_of():
        gathered = lax.all_gather(footprint_w, "roi", axis=0, tiled=True)
        return sum(
            jnp.where(hit[:, m, :].T[:, :, None], gathered[None, :, m, :], 0)
            for m in range(slot_count)
        ).astype(jnp.bfloat16)

    counts = jnp.minimum(jnp.arange(frames, dtype=jnp.int32) + 1, BASE_WIN)
    inverse = 1.0 / counts.astype(jnp.float32)
    middle = slab_width - LANES
    ids = jnp.stack([here, position]).astype(jnp.int32)
    if frames > BASE_WIN or devices % 4 or middle == 0:
        return plain_plan(
            movie, coeffs, dense_of, ids, inverse, here, position, devices, owners
        )

    far = list(range(devices - 1, devices // 2 - 1, -1))
    near = list(range(1, devices // 2))
    early, late = far[: len(far) // 2], far[len(far) // 2 :]

    def rows_of(source, k, low=0, high=slab_width):
        block = lax.dynamic_slice(
            source, (0, (here ^ k) * rows, low), (step, rows, high - low)
        )
        return block.reshape(step * rows, high - low)

    def send(block, k, *after):
        if after:
            block, *_ = lax.optimization_barrier((block, *after))
        return lax.ppermute(block, "tm", swaps(devices, k))

    opening = rows_of(movie, early[0])
    rest, opening = lax.optimization_barrier((movie, opening))
    whole = {early[0]: send(opening, early[0])}
    whole |= {k: send(rows_of(rest, k), k) for k in early[1:]}
    whole |= {k: send(rows_of(rest, k), k) for k in near}
    ties = [whole[near[0]]] + [whole[k] for k in early]
    low = {k: send(rows_of(rest, k, 0, middle), k, tie) for k, tie in zip(late, ties)}
    ties = ties[len(late) :] + list(low.values())
    high = {k: send(rows_of(rest, k, middle), k, tie) for k, tie in zip(late, ties)}
    whole[0] = rows_of(rest, 0)
    dense = dense_of()

    pixels, filtered, total = run_early(
        coeffs, dense, list(whole.values()), list(whole), frames, late
    )
    lower, total = run_late(
        coeffs[:, :, :middle],
        dense[:, :, :middle],
        total,
        pixels,
        low,
        owners,
        0,
        False,
    )
    pixels, filtered, lower, total = lax.optimization_barrier(
        (pixels, filtered, lower, total)
    )
    upper, *parts = run_late(
        coeffs[:, :, middle:],
        dense[:, :, middle:],
        total,
        pixels,
        high,
        owners,
        middle // LANES,
        True,
    )
    traces = parts[0]
    for k in range(1, owners):
        traces = traces + lax.ppermute(parts[k], "roi", swaps(owners, k))
    delta = run_delta(filtered, [lower, upper], late, rows, step)
    return delta, traces


def solution(mesh):
    placed = (
        P("tm", None, "roi"),
        P(None, "tm", "roi"),
        P(("tm", "roi"), None, None),
        P("tm", None),
        P("tm"),
    )
    return jax.shard_map(
        local,
        mesh=mesh,
        in_specs=placed,
        out_specs=(P(None, "tm", "roi"), P(("tm", "roi"), None)),
        check_vma=False,
    )
```

```python
import functools

import jax
import jax.numpy as jnp
from jax import lax
from jax.experimental import pallas as pl
from jax.experimental.pallas import tpu as pltpu
from jax.sharding import PartitionSpec as P

BASE_WIN = 128
LANES = 128


def chunk_kernel(
    ids_ref, inv_ref, coeff_ref, dense_ref, prev_ref, *rest, places, owners, last
):
    devices = len(places)
    parts = owners if last else 1
    blocks = rest[:devices]
    delta_ref = rest[devices]
    part_refs = rest[devices + 1 : devices + 1 + parts]
    pixels, filtered, delta32, partial = rest[devices + 1 + parts :]
    here = ids_ref[0]
    position = ids_ref[1]
    _, rows, width = pixels.shape
    step = blocks[0].shape[0]
    taps = coeff_ref.shape[0]
    frames = devices * step
    for block, (k, offset) in zip(blocks, places):
        start = pl.multiple_of((here ^ k) * step, step)
        pixels[pl.ds(start, step)] = block[:, :, offset : offset + width]

    for lane in range(0, width, LANES):
        span = slice(lane, lane + LANES)
        weights = [coeff_ref[k, :, span].astype(jnp.float32) for k in range(taps)]
        zero = jnp.zeros((rows, LANES), jnp.float32)

        def block_step(index, carry):
            running, history = carry[0], list(carry[1:])
            base = index * step
            for offset in range(step):
                frame = base + offset
                now = pixels[frame, :, span].astype(jnp.float32)
                total = weights[0] * now
                for k in range(1, taps):
                    total = total + weights[k] * history[k - 1]
                history = [now] + history[:-1]
                rounded = total.astype(jnp.bfloat16)
                value = rounded.astype(jnp.float32)
                running = running + value
                if frames > BASE_WIN:
                    filtered[frame, :, span] = rounded
                    gone = filtered[jnp.maximum(frame - BASE_WIN, 0), :, span]
                    running = running - jnp.where(
                        frame >= BASE_WIN, gone.astype(jnp.float32), 0.0
                    )
                delta = (value - running * inv_ref[frame]).astype(jnp.bfloat16)
                delta_ref[frame, :, span] = delta
                delta32[lane // LANES, pl.ds(frame * rows, rows), :] = delta.astype(
                    jnp.float32
                )
            return (running, *history)

        lax.fori_loop(0, devices, block_step, (zero,) * taps)

    total = prev_ref[...]
    for row in range(rows):
        picked = jnp.concatenate(
            [
                delta32[tile, pl.ds(row, frames, stride=rows), :].astype(jnp.bfloat16)
                for tile in range(width // LANES)
            ],
            axis=1,
        )
        total = total + lax.dot_general(
            dense_ref[row],
            picked,
            (((1,), (1,)), ((), ())),
            preferred_element_type=jnp.float32,
        )
    roi_here = total.shape[0] // owners
    if last:
        partial[...] = total.reshape(owners, roi_here, frames)
        for k in range(owners):
            part_refs[k][...] = partial[position ^ k]
    else:
        part_refs[0][...] = total


def run_chunk(ids, inverse, coeffs, dense, prev, blocks, places, owners, last):
    devices = len(blocks)
    step = blocks[0].shape[0]
    _, rows, width = coeffs.shape
    frames = devices * step
    rois = dense.shape[1]
    vmem = pl.BlockSpec(memory_space=pltpu.VMEM)
    smem = pl.BlockSpec(memory_space=pltpu.SMEM)
    held = frames if frames > BASE_WIN else 1
    parts = owners if last else 1
    return pl.pallas_call(
        functools.partial(chunk_kernel, places=tuple(places), owners=owners, last=last),
        out_shape=[jax.ShapeDtypeStruct((frames, rows, width), jnp.bfloat16)]
        + [jax.ShapeDtypeStruct((rois // parts, frames), jnp.float32)] * parts,
        in_specs=[smem, smem] + [vmem] * (3 + devices),
        out_specs=[vmem] * (1 + parts),
        scratch_shapes=[
            pltpu.VMEM((frames, rows, width), jnp.bfloat16),
            pltpu.VMEM((held, rows, width), jnp.bfloat16),
            pltpu.VMEM((width // LANES, (frames + 1) * rows, LANES), jnp.float32),
            pltpu.VMEM((owners, rois // owners, frames), jnp.float32),
        ],
        compiler_params=pltpu.CompilerParams(vmem_limit_bytes=24 * 1024 * 1024),
        cost_estimate=pl.CostEstimate(
            flops=2 * frames * rows * width * rois,
            bytes_accessed=4 * frames * rows * width,
            transcendentals=0,
        ),
    )(ids, inverse, coeffs, dense, prev, *blocks)


REACH = 8


def filtered_at(now, history, weights):
    total = weights[0] * now
    for tap in range(1, len(weights)):
        total = total + weights[tap] * history[tap - 1]
    return total.astype(jnp.bfloat16).astype(jnp.float32)


def tap_weights(coeff_ref, tile):
    span = slice(tile * LANES, (tile + 1) * LANES)
    return [coeff_ref[tap, :, span].astype(jnp.float32) for tap in range(coeff_ref.shape[0])]


def frame_rows(frame, rows):
    return pl.ds(pl.multiple_of(frame * rows, rows), rows)


def filter_rows(pixels, filtered, coeff_ref, frames, step):
    taps, rows, _ = coeff_ref.shape
    for tile in range(pixels.shape[0]):
        weights = tap_weights(coeff_ref, tile)

        def block_step(index, history):
            history = list(history)
            for offset in range(step):
                at = frame_rows(index * step + offset, rows)
                now = pixels[tile, at, :]
                filtered[tile, at, :] = filtered_at(now, history, weights)
                history = [now] + history[:-1]
            return tuple(history)

        zero = jnp.zeros((rows, LANES), jnp.float32)
        lax.fori_loop(0, frames // step, block_step, (zero,) * (taps - 1))


def project(filtered, dense_ref, first, frames):
    rows = dense_ref.shape[0]
    total = 0.0
    for row in range(rows):
        picked = jnp.concatenate(
            [
                filtered[tile, pl.ds(first * rows + row, frames, stride=rows), :].astype(
                    jnp.bfloat16
                )
                for tile in range(filtered.shape[0])
            ],
            axis=1,
        )
        total = total + lax.dot_general(
            dense_ref[row],
            picked,
            (((1,), (1,)), ((), ())),
            preferred_element_type=jnp.float32,
        )
    return total


def fill(pixels, blocks, places, here, step, rows):
    for block, (k, lane) in zip(blocks, places):
        start = pl.multiple_of((here ^ k) * (step * rows), step * rows)
        for tile in range(pixels.shape[0]):
            first = lane + tile * LANES
            pixels[tile, pl.ds(start, step * rows), :] = block[
                :, first : first + LANES
            ].astype(jnp.float32)


def late_frames(here, late, step):
    return (here ^ late[-1]) // len(late) * (len(late) * step), len(late) * step + REACH


def minus_mean(total):
    frames = total.shape[1]
    earlier = lax.broadcasted_iota(jnp.int32, (frames, frames), 0)
    later = lax.broadcasted_iota(jnp.int32, (frames, frames), 1)
    upto = jnp.where(earlier <= later, 1.0, 0.0).astype(jnp.bfloat16)
    high = total.astype(jnp.bfloat16)
    rest = total - high.astype(jnp.float32)
    middle = rest.astype(jnp.bfloat16)
    low = (rest - middle.astype(jnp.float32)).astype(jnp.bfloat16)
    running = sum(
        jnp.dot(term, upto, preferred_element_type=jnp.float32) for term in (low, middle, high)
    )
    frame_ids = lax.broadcasted_iota(jnp.int32, total.shape, 1)
    return total - running / jnp.minimum(frame_ids + 1, BASE_WIN).astype(jnp.float32)


def early_kernel(coeff_ref, dense_ref, *rest, places, step, frames, late):
    blocks = rest[: len(places)]
    pixels, filtered, total_ref = rest[len(places) :]
    rows = coeff_ref.shape[1]
    here = lax.axis_index("tm")
    first, length = late_frames(here, late, step)
    at = pl.ds(pl.multiple_of(first * rows, step * rows), length * rows)
    zeros = jnp.zeros((length * rows, LANES), jnp.float32)
    for tile in range(pixels.shape[0]):
        pixels[tile, at, :] = zeros
    fill(pixels, blocks, [(k, 0) for k in places], here, step, rows)
    filter_rows(pixels, filtered, coeff_ref, frames, step)
    for tile in range(pixels.shape[0]):
        filtered[tile, at, :] = zeros
    total_ref[...] = project(filtered, dense_ref, 0, frames)


def late_kernel(coeff_ref, dense_ref, total_ref, pixels, *rest, late, first_tile, last):
    blocks = rest[: len(late)]
    filtered, *outs, held, strip, partial = rest[len(late) :]
    here, position = lax.axis_index("tm"), lax.axis_index("roi")
    taps, rows, width = coeff_ref.shape
    step = blocks[0].shape[0] // rows
    frames = total_ref.shape[1]
    first, length = late_frames(here, late, step)
    for tile in range(width // LANES):
        own = pixels.at[first_tile + tile]
        for block, k in zip(blocks, late):
            start = pl.multiple_of(((here ^ k) * step - first) * rows, step * rows)
            held[pl.ds(start, step * rows), :] = block[
                :, tile * LANES : (tile + 1) * LANES
            ].astype(jnp.float32)
        after = pl.multiple_of((first + length - REACH) * rows, step * rows)
        held[pl.ds((length - REACH) * rows, REACH * rows), :] = own[pl.ds(after, REACH * rows), :]
        weights = tap_weights(coeff_ref, tile)
        history = []
        for tap in range(1, taps):
            earlier = own[frame_rows(jnp.maximum(first - tap, 0), rows), :]
            history.append(jnp.where(first > 0, earlier, 0.0))

        def block_step(index, history):
            history = list(history)
            for offset in range(REACH):
                at = frame_rows(index * REACH + offset, rows)
                now = held[at, :]
                filtered[tile, at, :] = filtered_at(now, history, weights)
                history = [now] + history[:-1]
            return tuple(history)

        lax.fori_loop(0, length // REACH, block_step, tuple(history))
    strip[...] = jnp.zeros(strip.shape, jnp.float32)
    strip[:, :length] = project(filtered, dense_ref, 0, length)
    frame_ids = lax.broadcasted_iota(jnp.int32, strip.shape, 1)
    found = jnp.where(frame_ids < frames - first, strip[...], 0.0)
    total = total_ref[...] + pltpu.roll(found, first, 1)
    if last:
        partial[...] = minus_mean(total).reshape(partial.shape)
        for k, out in enumerate(outs):
            out[...] = partial[position ^ k]
    else:
        outs[0][...] = total


def delta_kernel(*rest, late, step):
    *pieces, filtered, out_ref, inv_ref, packed, sems = rest
    tiles, frames, rows, _ = packed.shape
    first, length = late_frames(lax.axis_index("tm"), late, step)
    end = jnp.minimum(first + length, frames)
    counts = lax.broadcasted_iota(jnp.int32, (frames, LANES), 0) + 1
    inv_ref[...] = 1.0 / jnp.minimum(counts, BASE_WIN).astype(jnp.float32)
    places = [(piece, tile) for piece in pieces[::-1] for tile in range(piece.shape[0])]
    copies = []
    for tile in range(0, tiles, 2):
        several = range(tile, min(tile + 2, tiles))

        def subtract_mean(source, low, high, running):
            def block_step(index, running):
                running = list(running)
                for offset in range(REACH):
                    frame = index * REACH + offset
                    for turn, one in enumerate(several):
                        value = source(one, frame)
                        running[turn] = running[turn] + value
                        packed[one, frame] = (value - running[turn] * inv_ref[pl.ds(frame, 1), :]).astype(
                            jnp.bfloat16
                        )
                return tuple(running)

            return lax.fori_loop(low // REACH, high // REACH, block_step, running)

        def early(one, frame):
            return filtered[one, frame_rows(frame, rows), :]

        def middle(one, frame):
            piece, its_tile = places[one]
            return piece[its_tile, frame_rows(frame - first, rows), :]

        zero = jnp.zeros((rows, LANES), jnp.float32)
        running = subtract_mean(early, 0, first, (zero,) * len(several))
        running = subtract_mean(middle, first, end, running)
        subtract_mean(early, end, frames, running)
        for one in several:
            place = out_ref.at[:, :, pl.ds(one * LANES, LANES)]
            copies.append(pltpu.make_async_copy(packed.at[one], place, sems.at[one]))
            copies[-1].start()
    for copy in copies:
        copy.wait()


VMEM = pl.BlockSpec(memory_space=pltpu.VMEM)
SMEM = pl.BlockSpec(memory_space=pltpu.SMEM)
ANYWHERE = pl.BlockSpec(memory_space=pl.ANY)


def options(mib, work):
    return dict(
        compiler_params=pltpu.CompilerParams(vmem_limit_bytes=mib * 1024 * 1024),
        cost_estimate=pl.CostEstimate(flops=16 * work, bytes_accessed=4 * work, transcendentals=0),
    )


def run_early(coeffs, dense, blocks, places, frames, late):
    _, rows, width = coeffs.shape
    step = blocks[0].shape[0] // rows
    held = jax.ShapeDtypeStruct((width // LANES, (frames + 2 * REACH) * rows, LANES), jnp.float32)
    return pl.pallas_call(
        functools.partial(
            early_kernel, places=tuple(places), step=step, frames=frames, late=tuple(late)
        ),
        out_shape=[held, held, jax.ShapeDtypeStruct((dense.shape[1], frames), jnp.float32)],
        in_specs=[VMEM] * (2 + len(blocks)),
        out_specs=[VMEM] * 3,
        **options(4, frames * rows * width),
    )(coeffs, dense, *blocks)


def run_late(coeffs, dense, total, pixels, late, owners, first_tile, last):
    _, rows, width = coeffs.shape
    rois, frames = total.shape
    height = sum(block.shape[0] for block in late.values()) + (REACH + 1) * rows
    parts = owners if last else 1
    part = jax.ShapeDtypeStruct((rois // parts, frames), jnp.float32)
    return pl.pallas_call(
        functools.partial(late_kernel, late=tuple(late), first_tile=first_tile, last=last),
        out_shape=[jax.ShapeDtypeStruct((width // LANES, height, LANES), jnp.float32)]
        + [part] * parts,
        in_specs=[VMEM] * (4 + len(late)),
        out_specs=[VMEM] * (1 + parts),
        scratch_shapes=[
            pltpu.VMEM((height, LANES), jnp.float32),
            pltpu.VMEM((rois, frames), jnp.float32),
            pltpu.VMEM((owners, rois // owners, frames), jnp.float32),
        ],
        **options(4, frames * rows * width),
    )(coeffs, dense, total, pixels, *late.values())


def run_delta(filtered, pieces, late, rows, step):
    tiles, frames = filtered.shape[0], filtered.shape[1] // rows - 2 * REACH
    return pl.pallas_call(
        functools.partial(delta_kernel, late=tuple(late), step=step),
        out_shape=jax.ShapeDtypeStruct((frames, rows, tiles * LANES), jnp.bfloat16),
        in_specs=[VMEM] * (1 + len(pieces)),
        out_specs=ANYWHERE,
        scratch_shapes=[
            pltpu.VMEM((frames, LANES), jnp.float32),
            pltpu.VMEM((tiles, frames, rows, LANES), jnp.bfloat16),
            pltpu.SemaphoreType.DMA((tiles,)),
        ],
        **options(4, frames * rows * tiles * LANES),
    )(*pieces[::-1], filtered)


def swaps(count, k):
    return [(i, i ^ k) for i in range(count)]


def plain_plan(movie, coeffs, dense_of, ids, inverse, here, position, devices, owners):
    step, _, slab_width = movie.shape
    rows = coeffs.shape[1]
    frames = devices * step
    middle = slab_width // LANES // 2 * LANES
    cuts = [0, middle, slab_width]
    near = list(range(devices // 2 - 1, 0, -1))
    far = list(range(devices - 1, devices // 2 - 1, -1))
    split = far[len(far) // 2 :]
    opening = [(k, 0, slab_width) for k in far[: len(far) // 2]]
    beside = [(k, 0, slab_width) for k in near]
    first = [(k, 0, middle) for k in split]
    second = [(k, middle, slab_width) for k in split]
    ties = dict(zip(first + second, beside[::-1][: len(first) - 1] + opening + first))

    def rows_of(source, k, low, high):
        return lax.dynamic_slice(source, (0, (here ^ k) * rows, low), (step, rows, high - low))

    blocks = [rows_of(movie, *item) for item in opening]
    rest, *blocks = lax.optimization_barrier((movie, *blocks))
    arrived = {}
    for item in opening + beside + first + second:
        block = blocks.pop(0) if blocks else rows_of(rest, *item)
        if item in ties:
            block, arrived[ties[item]] = lax.optimization_barrier((block, arrived[ties[item]]))
        arrived[item] = lax.ppermute(block, "tm", swaps(devices, item[0]))
    arrived[0, 0, slab_width] = rows_of(rest, 0, 0, slab_width)
    chunks = []
    for low, high in zip(cuts[:-1], cuts[1:]):
        chunks.append(
            [
                (block, (k, low - start))
                for (k, start, end), block in arrived.items()
                if start <= low and high <= end
            ]
        )

    dense = dense_of()
    prev = jnp.zeros((dense.shape[1], frames), jnp.float32)
    deltas = []
    for low, high, received in zip(cuts[:-1], cuts[1:], chunks):
        delta, *parts = run_chunk(
            ids,
            inverse,
            coeffs[:, :, low:high],
            dense[:, :, low:high],
            prev,
            [block for block, _ in received],
            [place for _, place in received],
            owners,
            high == slab_width,
        )
        deltas.append(delta)
        prev = parts[0]
    traces = parts[0]
    for k in range(1, owners):
        traces = traces + lax.ppermute(parts[k], "roi", swaps(owners, k))
    return jnp.concatenate(deltas, axis=2), traces


def local(movie, coeffs, footprint_w, roi_blocks, roi_len):
    devices = lax.axis_size("tm")
    owners = lax.axis_size("roi")
    here = lax.axis_index("tm")
    position = lax.axis_index("roi")
    step, _, slab_width = movie.shape
    rows = coeffs.shape[1]
    frames = devices * step
    slot_count = roi_blocks.shape[1]

    live = jnp.arange(slot_count, dtype=jnp.int32)[None, :] < roi_len[:, None]
    live = live & (roi_blocks // rows == position)
    hit = live[:, :, None] & (
        (roi_blocks % rows)[:, :, None] == jnp.arange(rows, dtype=jnp.int32)
    )

    def dense_of():
        gathered = lax.all_gather(footprint_w, "roi", axis=0, tiled=True)
        return sum(
            jnp.where(hit[:, m, :].T[:, :, None], gathered[None, :, m, :], 0)
            for m in range(slot_count)
        ).astype(jnp.bfloat16)

    counts = jnp.minimum(jnp.arange(frames, dtype=jnp.int32) + 1, BASE_WIN)
    inverse = 1.0 / counts.astype(jnp.float32)
    middle = slab_width - LANES
    ids = jnp.stack([here, position]).astype(jnp.int32)
    if frames > BASE_WIN or devices % 4 or middle == 0:
        return plain_plan(
            movie, coeffs, dense_of, ids, inverse, here, position, devices, owners
        )

    far = list(range(devices - 1, devices // 2 - 1, -1))
    near = list(range(1, devices // 2))
    early, late = far[: len(far) // 2], far[len(far) // 2 :]

    def rows_of(source, k, low=0, high=slab_width):
        block = lax.dynamic_slice(
            source, (0, (here ^ k) * rows, low), (step, rows, high - low)
        )
        return block.reshape(step * rows, high - low)

    def send(block, k, *after):
        if after:
            block, *_ = lax.optimization_barrier((block, *after))
        return lax.ppermute(block, "tm", swaps(devices, k))

    opening = rows_of(movie, early[0])
    rest, opening = lax.optimization_barrier((movie, opening))
    whole = {early[0]: send(opening, early[0])}
    whole |= {k: send(rows_of(rest, k), k) for k in early[1:]}
    whole |= {k: send(rows_of(rest, k), k) for k in near}
    ties = [whole[near[0]]] + [whole[k] for k in early]
    low = {k: send(rows_of(rest, k, 0, middle), k, tie) for k, tie in zip(late, ties)}
    ties = ties[len(late) :] + list(low.values())
    high = {k: send(rows_of(rest, k, middle), k, tie) for k, tie in zip(late, ties)}
    whole[0] = rows_of(rest, 0)
    dense = dense_of()

    pixels, filtered, total = run_early(
        coeffs, dense, list(whole.values()), list(whole), frames, late
    )
    lower, total = run_late(
        coeffs[:, :, :middle],
        dense[:, :, :middle],
        total,
        pixels,
        low,
        owners,
        0,
        False,
    )
    pixels, filtered, lower, total = lax.optimization_barrier(
        (pixels, filtered, lower, total)
    )
    upper, *parts = run_late(
        coeffs[:, :, middle:],
        dense[:, :, middle:],
        total,
        pixels,
        high,
        owners,
        middle // LANES,
        True,
    )
    traces = parts[0]
    for k in range(1, owners):
        traces = traces + lax.ppermute(parts[k], "roi", swaps(owners, k))
    delta = run_delta(filtered, [lower, upper], late, rows, step)
    return delta, traces


def solution(mesh):
    placed = (
        P("tm", None, "roi"),
        P(None, "tm", "roi"),
        P(("tm", "roi"), None, None),
        P("tm", None),
        P("tm"),
    )
    return jax.shard_map(
        local,
        mesh=mesh,
        in_specs=placed,
        out_specs=(P(None, "tm", "roi"), P(("tm", "roi"), None)),
        check_vma=False,
    )
```

```python
import functools

import jax
import jax.numpy as jnp
from jax import lax
from jax.experimental import pallas as pl
from jax.experimental.pallas import tpu as pltpu
from jax.sharding import PartitionSpec as P

BASE_WIN = 128
LANES = 128


def chunk_kernel(
    ids_ref, inv_ref, coeff_ref, dense_ref, prev_ref, *rest, places, owners, last
):
    devices = len(places)
    parts = owners if last else 1
    blocks = rest[:devices]
    delta_ref = rest[devices]
    part_refs = rest[devices + 1 : devices + 1 + parts]
    pixels, filtered, delta32, partial = rest[devices + 1 + parts :]
    here = ids_ref[0]
    position = ids_ref[1]
    _, rows, width = pixels.shape
    step = blocks[0].shape[0]
    taps = coeff_ref.shape[0]
    frames = devices * step
    for block, (k, offset) in zip(blocks, places):
        start = pl.multiple_of((here ^ k) * step, step)
        pixels[pl.ds(start, step)] = block[:, :, offset : offset + width]

    for lane in range(0, width, LANES):
        span = slice(lane, lane + LANES)
        weights = [coeff_ref[k, :, span].astype(jnp.float32) for k in range(taps)]
        zero = jnp.zeros((rows, LANES), jnp.float32)

        def block_step(index, carry):
            running, history = carry[0], list(carry[1:])
            base = index * step
            for offset in range(step):
                frame = base + offset
                now = pixels[frame, :, span].astype(jnp.float32)
                total = weights[0] * now
                for k in range(1, taps):
                    total = total + weights[k] * history[k - 1]
                history = [now] + history[:-1]
                rounded = total.astype(jnp.bfloat16)
                value = rounded.astype(jnp.float32)
                running = running + value
                if frames > BASE_WIN:
                    filtered[frame, :, span] = rounded
                    gone = filtered[jnp.maximum(frame - BASE_WIN, 0), :, span]
                    running = running - jnp.where(
                        frame >= BASE_WIN, gone.astype(jnp.float32), 0.0
                    )
                delta = (value - running * inv_ref[frame]).astype(jnp.bfloat16)
                delta_ref[frame, :, span] = delta
                delta32[lane // LANES, pl.ds(frame * rows, rows), :] = delta.astype(
                    jnp.float32
                )
            return (running, *history)

        lax.fori_loop(0, devices, block_step, (zero,) * taps)

    total = prev_ref[...]
    for row in range(rows):
        picked = jnp.concatenate(
            [
                delta32[tile, pl.ds(row, frames, stride=rows), :].astype(jnp.bfloat16)
                for tile in range(width // LANES)
            ],
            axis=1,
        )
        total = total + lax.dot_general(
            dense_ref[row],
            picked,
            (((1,), (1,)), ((), ())),
            preferred_element_type=jnp.float32,
        )
    roi_here = total.shape[0] // owners
    if last:
        partial[...] = total.reshape(owners, roi_here, frames)
        for k in range(owners):
            part_refs[k][...] = partial[position ^ k]
    else:
        part_refs[0][...] = total


def run_chunk(ids, inverse, coeffs, dense, prev, blocks, places, owners, last):
    devices = len(blocks)
    step = blocks[0].shape[0]
    _, rows, width = coeffs.shape
    frames = devices * step
    rois = dense.shape[1]
    vmem = pl.BlockSpec(memory_space=pltpu.VMEM)
    smem = pl.BlockSpec(memory_space=pltpu.SMEM)
    held = frames if frames > BASE_WIN else 1
    parts = owners if last else 1
    return pl.pallas_call(
        functools.partial(chunk_kernel, places=tuple(places), owners=owners, last=last),
        out_shape=[jax.ShapeDtypeStruct((frames, rows, width), jnp.bfloat16)]
        + [jax.ShapeDtypeStruct((rois // parts, frames), jnp.float32)] * parts,
        in_specs=[smem, smem] + [vmem] * (3 + devices),
        out_specs=[vmem] * (1 + parts),
        scratch_shapes=[
            pltpu.VMEM((frames, rows, width), jnp.bfloat16),
            pltpu.VMEM((held, rows, width), jnp.bfloat16),
            pltpu.VMEM((width // LANES, (frames + 1) * rows, LANES), jnp.float32),
            pltpu.VMEM((owners, rois // owners, frames), jnp.float32),
        ],
        compiler_params=pltpu.CompilerParams(vmem_limit_bytes=24 * 1024 * 1024),
        cost_estimate=pl.CostEstimate(
            flops=2 * frames * rows * width * rois,
            bytes_accessed=4 * frames * rows * width,
            transcendentals=0,
        ),
    )(ids, inverse, coeffs, dense, prev, *blocks)


REACH = 8


def filtered_at(now, history, weights):
    total = weights[0] * now
    for tap in range(1, len(weights)):
        total = total + weights[tap] * history[tap - 1]
    return total.astype(jnp.bfloat16).astype(jnp.float32)


def tap_weights(coeff_ref, tile):
    span = slice(tile * LANES, (tile + 1) * LANES)
    return [coeff_ref[tap, :, span].astype(jnp.float32) for tap in range(coeff_ref.shape[0])]


def frame_rows(frame, rows):
    return pl.ds(pl.multiple_of(frame * rows, rows), rows)


def filter_rows(pixels, filtered, coeff_ref, frames, step):
    taps, rows, _ = coeff_ref.shape
    for tile in range(pixels.shape[0]):
        weights = tap_weights(coeff_ref, tile)

        def block_step(index, history):
            history = list(history)
            for offset in range(step):
                at = frame_rows(index * step + offset, rows)
                now = pixels[tile, at, :]
                filtered[tile, at, :] = filtered_at(now, history, weights)
                history = [now] + history[:-1]
            return tuple(history)

        zero = jnp.zeros((rows, LANES), jnp.float32)
        lax.fori_loop(0, frames // step, block_step, (zero,) * (taps - 1))


def project(filtered, dense_ref, first, frames):
    rows, tiles = dense_ref.shape[0], filtered.shape[0]
    joined = max(1, 256 // (tiles * LANES))
    total = 0.0
    for row in range(0, rows, joined):
        several = range(row, min(row + joined, rows))
        picked = [
            filtered[tile, pl.ds(first * rows + one, frames, stride=rows), :].astype(jnp.bfloat16)
            for one in several
            for tile in range(tiles)
        ]
        total = total + lax.dot_general(
            jnp.concatenate([dense_ref[one] for one in several], axis=1),
            jnp.concatenate(picked, axis=1),
            (((1,), (1,)), ((), ())),
            preferred_element_type=jnp.float32,
        )
    return total


def fill(pixels, blocks, places, here, step, rows):
    for block, (k, lane) in zip(blocks, places):
        start = pl.multiple_of((here ^ k) * (step * rows), step * rows)
        for tile in range(pixels.shape[0]):
            first = lane + tile * LANES
            pixels[tile, pl.ds(start, step * rows), :] = block[
                :, first : first + LANES
            ].astype(jnp.float32)


def late_frames(here, late, step):
    return (here ^ late[-1]) // len(late) * (len(late) * step), len(late) * step + REACH


def minus_mean(total):
    frames = total.shape[1]
    earlier = lax.broadcasted_iota(jnp.int32, (frames, frames), 0)
    later = lax.broadcasted_iota(jnp.int32, (frames, frames), 1)
    upto = jnp.where(earlier <= later, 1.0, 0.0).astype(jnp.bfloat16)
    high = total.astype(jnp.bfloat16)
    rest = total - high.astype(jnp.float32)
    middle = rest.astype(jnp.bfloat16)
    low = (rest - middle.astype(jnp.float32)).astype(jnp.bfloat16)
    running = sum(
        jnp.dot(term, upto, preferred_element_type=jnp.float32) for term in (low, middle, high)
    )
    frame_ids = lax.broadcasted_iota(jnp.int32, total.shape, 1)
    return total - running / jnp.minimum(frame_ids + 1, BASE_WIN).astype(jnp.float32)


def early_kernel(coeff_ref, dense_ref, *rest, places, step, frames, late):
    blocks = rest[: len(places)]
    pixels, filtered, total_ref = rest[len(places) :]
    rows = coeff_ref.shape[1]
    here = lax.axis_index("tm")
    first, length = late_frames(here, late, step)
    at = pl.ds(pl.multiple_of(first * rows, step * rows), length * rows)
    zeros = jnp.zeros((length * rows, LANES), jnp.float32)
    for tile in range(pixels.shape[0]):
        pixels[tile, at, :] = zeros
    fill(pixels, blocks, [(k, 0) for k in places], here, step, rows)
    filter_rows(pixels, filtered, coeff_ref, frames, step)
    for tile in range(pixels.shape[0]):
        filtered[tile, at, :] = zeros
    total_ref[...] = project(filtered, dense_ref, 0, frames)


def late_kernel(coeff_ref, dense_ref, total_ref, pixels, *rest, late, first_tile, last):
    blocks = rest[: len(late)]
    filtered, *outs, held, strip, partial = rest[len(late) :]
    here, position = lax.axis_index("tm"), lax.axis_index("roi")
    taps, rows, width = coeff_ref.shape
    step = blocks[0].shape[0] // rows
    frames = total_ref.shape[1]
    first, length = late_frames(here, late, step)
    for tile in range(width // LANES):
        own = pixels.at[first_tile + tile]
        for block, k in zip(blocks, late):
            start = pl.multiple_of(((here ^ k) * step - first) * rows, step * rows)
            held[pl.ds(start, step * rows), :] = block[
                :, tile * LANES : (tile + 1) * LANES
            ].astype(jnp.float32)
        after = pl.multiple_of((first + length - REACH) * rows, step * rows)
        held[pl.ds((length - REACH) * rows, REACH * rows), :] = own[pl.ds(after, REACH * rows), :]
        weights = tap_weights(coeff_ref, tile)
        history = []
        for tap in range(1, taps):
            earlier = own[frame_rows(jnp.maximum(first - tap, 0), rows), :]
            history.append(jnp.where(first > 0, earlier, 0.0))

        def block_step(index, history):
            history = list(history)
            for offset in range(REACH):
                at = frame_rows(index * REACH + offset, rows)
                now = held[at, :]
                filtered[tile, at, :] = filtered_at(now, history, weights)
                history = [now] + history[:-1]
            return tuple(history)

        lax.fori_loop(0, length // REACH, block_step, tuple(history))
    strip[...] = jnp.zeros(strip.shape, jnp.float32)
    strip[:, :length] = project(filtered, dense_ref, 0, length)
    frame_ids = lax.broadcasted_iota(jnp.int32, strip.shape, 1)
    found = jnp.where(frame_ids < frames - first, strip[...], 0.0)
    total = total_ref[...] + pltpu.roll(found, first, 1)
    if last:
        partial[...] = minus_mean(total).reshape(partial.shape)
        for k, out in enumerate(outs):
            out[...] = partial[position ^ k]
    else:
        outs[0][...] = total


def delta_kernel(*rest, late, step):
    *pieces, filtered, out_ref, inv_ref, packed, sems = rest
    tiles, frames, rows, _ = packed.shape
    first, length = late_frames(lax.axis_index("tm"), late, step)
    end = jnp.minimum(first + length, frames)
    counts = lax.broadcasted_iota(jnp.int32, (frames, LANES), 0) + 1
    inv_ref[...] = 1.0 / jnp.minimum(counts, BASE_WIN).astype(jnp.float32)
    places = [(piece, tile) for piece in pieces[::-1] for tile in range(piece.shape[0])]
    copies = []
    for tile in range(0, tiles, 2):
        several = range(tile, min(tile + 2, tiles))

        def subtract_mean(source, low, high, running):
            def block_step(index, running):
                running = list(running)
                for offset in range(REACH):
                    frame = index * REACH + offset
                    for turn, one in enumerate(several):
                        value = source(one, frame)
                        running[turn] = running[turn] + value
                        packed[one, frame] = (value - running[turn] * inv_ref[pl.ds(frame, 1), :]).astype(
                            jnp.bfloat16
                        )
                return tuple(running)

            return lax.fori_loop(low // REACH, high // REACH, block_step, running)

        def early(one, frame):
            return filtered[one, frame_rows(frame, rows), :]

        def middle(one, frame):
            piece, its_tile = places[one]
            return piece[its_tile, frame_rows(frame - first, rows), :]

        zero = jnp.zeros((rows, LANES), jnp.float32)
        running = subtract_mean(early, 0, first, (zero,) * len(several))
        running = subtract_mean(middle, first, end, running)
        subtract_mean(early, end, frames, running)
        for one in several:
            place = out_ref.at[:, :, pl.ds(one * LANES, LANES)]
            copies.append(pltpu.make_async_copy(packed.at[one], place, sems.at[one]))
            copies[-1].start()
    for copy in copies:
        copy.wait()


VMEM = pl.BlockSpec(memory_space=pltpu.VMEM)
SMEM = pl.BlockSpec(memory_space=pltpu.SMEM)
ANYWHERE = pl.BlockSpec(memory_space=pl.ANY)


def options(mib, work):
    return dict(
        compiler_params=pltpu.CompilerParams(vmem_limit_bytes=mib * 1024 * 1024),
        cost_estimate=pl.CostEstimate(flops=16 * work, bytes_accessed=4 * work, transcendentals=0),
    )


def run_early(coeffs, dense, blocks, places, frames, late):
    _, rows, width = coeffs.shape
    step = blocks[0].shape[0] // rows
    held = jax.ShapeDtypeStruct((width // LANES, (frames + 2 * REACH) * rows, LANES), jnp.float32)
    return pl.pallas_call(
        functools.partial(
            early_kernel, places=tuple(places), step=step, frames=frames, late=tuple(late)
        ),
        out_shape=[held, held, jax.ShapeDtypeStruct((dense.shape[1], frames), jnp.float32)],
        in_specs=[VMEM] * (2 + len(blocks)),
        out_specs=[VMEM] * 3,
        **options(4, frames * rows * width),
    )(coeffs, dense, *blocks)


def run_late(coeffs, dense, total, pixels, late, owners, first_tile, last):
    _, rows, width = coeffs.shape
    rois, frames = total.shape
    height = sum(block.shape[0] for block in late.values()) + (REACH + 1) * rows
    parts = owners if last else 1
    part = jax.ShapeDtypeStruct((rois // parts, frames), jnp.float32)
    return pl.pallas_call(
        functools.partial(late_kernel, late=tuple(late), first_tile=first_tile, last=last),
        out_shape=[jax.ShapeDtypeStruct((width // LANES, height, LANES), jnp.float32)]
        + [part] * parts,
        in_specs=[VMEM] * (4 + len(late)),
        out_specs=[VMEM] * (1 + parts),
        scratch_shapes=[
            pltpu.VMEM((height, LANES), jnp.float32),
            pltpu.VMEM((rois, frames), jnp.float32),
            pltpu.VMEM((owners, rois // owners, frames), jnp.float32),
        ],
        **options(4, frames * rows * width),
    )(coeffs, dense, total, pixels, *late.values())


def run_delta(filtered, pieces, late, rows, step):
    tiles, frames = filtered.shape[0], filtered.shape[1] // rows - 2 * REACH
    return pl.pallas_call(
        functools.partial(delta_kernel, late=tuple(late), step=step),
        out_shape=jax.ShapeDtypeStruct((frames, rows, tiles * LANES), jnp.bfloat16),
        in_specs=[VMEM] * (1 + len(pieces)),
        out_specs=ANYWHERE,
        scratch_shapes=[
            pltpu.VMEM((frames, LANES), jnp.float32),
            pltpu.VMEM((tiles, frames, rows, LANES), jnp.bfloat16),
            pltpu.SemaphoreType.DMA((tiles,)),
        ],
        **options(4, frames * rows * tiles * LANES),
    )(*pieces[::-1], filtered)


def swaps(count, k):
    return [(i, i ^ k) for i in range(count)]


def plain_plan(movie, coeffs, dense_of, ids, inverse, here, position, devices, owners):
    step, _, slab_width = movie.shape
    rows = coeffs.shape[1]
    frames = devices * step
    middle = slab_width // LANES // 2 * LANES
    cuts = [0, middle, slab_width]
    near = list(range(devices // 2 - 1, 0, -1))
    far = list(range(devices - 1, devices // 2 - 1, -1))
    split = far[len(far) // 2 :]
    opening = [(k, 0, slab_width) for k in far[: len(far) // 2]]
    beside = [(k, 0, slab_width) for k in near]
    first = [(k, 0, middle) for k in split]
    second = [(k, middle, slab_width) for k in split]
    ties = dict(zip(first + second, beside[::-1][: len(first) - 1] + opening + first))

    def rows_of(source, k, low, high):
        return lax.dynamic_slice(source, (0, (here ^ k) * rows, low), (step, rows, high - low))

    blocks = [rows_of(movie, *item) for item in opening]
    rest, *blocks = lax.optimization_barrier((movie, *blocks))
    arrived = {}
    for item in opening + beside + first + second:
        block = blocks.pop(0) if blocks else rows_of(rest, *item)
        if item in ties:
            block, arrived[ties[item]] = lax.optimization_barrier((block, arrived[ties[item]]))
        arrived[item] = lax.ppermute(block, "tm", swaps(devices, item[0]))
    arrived[0, 0, slab_width] = rows_of(rest, 0, 0, slab_width)
    chunks = []
    for low, high in zip(cuts[:-1], cuts[1:]):
        chunks.append(
            [
                (block, (k, low - start))
                for (k, start, end), block in arrived.items()
                if start <= low and high <= end
            ]
        )

    dense = dense_of()
    prev = jnp.zeros((dense.shape[1], frames), jnp.float32)
    deltas = []
    for low, high, received in zip(cuts[:-1], cuts[1:], chunks):
        delta, *parts = run_chunk(
            ids,
            inverse,
            coeffs[:, :, low:high],
            dense[:, :, low:high],
            prev,
            [block for block, _ in received],
            [place for _, place in received],
            owners,
            high == slab_width,
        )
        deltas.append(delta)
        prev = parts[0]
    traces = parts[0]
    for k in range(1, owners):
        traces = traces + lax.ppermute(parts[k], "roi", swaps(owners, k))
    return jnp.concatenate(deltas, axis=2), traces


def local(movie, coeffs, footprint_w, roi_blocks, roi_len):
    devices = lax.axis_size("tm")
    owners = lax.axis_size("roi")
    here = lax.axis_index("tm")
    position = lax.axis_index("roi")
    step, _, slab_width = movie.shape
    rows = coeffs.shape[1]
    frames = devices * step
    slot_count = roi_blocks.shape[1]

    live = jnp.arange(slot_count, dtype=jnp.int32)[None, :] < roi_len[:, None]
    live = live & (roi_blocks // rows == position)
    hit = live[:, :, None] & (
        (roi_blocks % rows)[:, :, None] == jnp.arange(rows, dtype=jnp.int32)
    )

    def dense_of():
        gathered = lax.all_gather(footprint_w, "roi", axis=0, tiled=True)
        return sum(
            jnp.where(hit[:, m, :].T[:, :, None], gathered[None, :, m, :], 0)
            for m in range(slot_count)
        ).astype(jnp.bfloat16)

    counts = jnp.minimum(jnp.arange(frames, dtype=jnp.int32) + 1, BASE_WIN)
    inverse = 1.0 / counts.astype(jnp.float32)
    middle = slab_width - LANES
    ids = jnp.stack([here, position]).astype(jnp.int32)
    if frames > BASE_WIN or devices % 4 or middle == 0:
        return plain_plan(
            movie, coeffs, dense_of, ids, inverse, here, position, devices, owners
        )

    far = list(range(devices - 1, devices // 2 - 1, -1))
    near = list(range(1, devices // 2))
    early, late = far[: len(far) // 2], far[len(far) // 2 :]

    def rows_of(source, k, low=0, high=slab_width):
        block = lax.dynamic_slice(
            source, (0, (here ^ k) * rows, low), (step, rows, high - low)
        )
        return block.reshape(step * rows, high - low)

    def send(block, k, *after):
        if after:
            block, *_ = lax.optimization_barrier((block, *after))
        return lax.ppermute(block, "tm", swaps(devices, k))

    opening = rows_of(movie, early[0])
    rest, opening = lax.optimization_barrier((movie, opening))
    whole = {early[0]: send(opening, early[0])}
    whole |= {k: send(rows_of(rest, k), k) for k in early[1:]}
    whole |= {k: send(rows_of(rest, k), k) for k in near}
    ties = [whole[near[0]]] + [whole[k] for k in early]
    low = {k: send(rows_of(rest, k, 0, middle), k, tie) for k, tie in zip(late, ties)}
    ties = ties[len(late) :] + list(low.values())
    high = {k: send(rows_of(rest, k, middle), k, tie) for k, tie in zip(late, ties)}
    whole[0] = rows_of(rest, 0)
    dense = dense_of()

    pixels, filtered, total = run_early(
        coeffs, dense, list(whole.values()), list(whole), frames, late
    )
    lower, total = run_late(
        coeffs[:, :, :middle],
        dense[:, :, :middle],
        total,
        pixels,
        low,
        owners,
        0,
        False,
    )
    pixels, filtered, lower, total = lax.optimization_barrier(
        (pixels, filtered, lower, total)
    )
    upper, *parts = run_late(
        coeffs[:, :, middle:],
        dense[:, :, middle:],
        total,
        pixels,
        high,
        owners,
        middle // LANES,
        True,
    )
    traces = parts[0]
    for k in range(1, owners):
        traces = traces + lax.ppermute(parts[k], "roi", swaps(owners, k))
    delta = run_delta(filtered, [lower, upper], late, rows, step)
    return delta, traces


def solution(mesh):
    placed = (
        P("tm", None, "roi"),
        P(None, "tm", "roi"),
        P(("tm", "roi"), None, None),
        P("tm", None),
        P("tm"),
    )
    return jax.shard_map(
        local,
        mesh=mesh,
        in_specs=placed,
        out_specs=(P(None, "tm", "roi"), P(("tm", "roi"), None)),
        check_vma=False,
    )
```

```python
import functools

import jax
import jax.numpy as jnp
from jax import lax
from jax.experimental import pallas as pl
from jax.experimental.pallas import tpu as pltpu
from jax.sharding import PartitionSpec as P

BASE_WIN = 128
LANES = 128


def chunk_kernel(
    ids_ref, inv_ref, coeff_ref, dense_ref, prev_ref, *rest, places, owners, last
):
    devices = len(places)
    parts = owners if last else 1
    blocks = rest[:devices]
    delta_ref = rest[devices]
    part_refs = rest[devices + 1 : devices + 1 + parts]
    pixels, filtered, delta32, partial = rest[devices + 1 + parts :]
    here = ids_ref[0]
    position = ids_ref[1]
    _, rows, width = pixels.shape
    step = blocks[0].shape[0]
    taps = coeff_ref.shape[0]
    frames = devices * step
    for block, (k, offset) in zip(blocks, places):
        start = pl.multiple_of((here ^ k) * step, step)
        pixels[pl.ds(start, step)] = block[:, :, offset : offset + width]

    for lane in range(0, width, LANES):
        span = slice(lane, lane + LANES)
        weights = [coeff_ref[k, :, span].astype(jnp.float32) for k in range(taps)]
        zero = jnp.zeros((rows, LANES), jnp.float32)

        def block_step(index, carry):
            running, history = carry[0], list(carry[1:])
            base = index * step
            for offset in range(step):
                frame = base + offset
                now = pixels[frame, :, span].astype(jnp.float32)
                total = weights[0] * now
                for k in range(1, taps):
                    total = total + weights[k] * history[k - 1]
                history = [now] + history[:-1]
                rounded = total.astype(jnp.bfloat16)
                value = rounded.astype(jnp.float32)
                running = running + value
                if frames > BASE_WIN:
                    filtered[frame, :, span] = rounded
                    gone = filtered[jnp.maximum(frame - BASE_WIN, 0), :, span]
                    running = running - jnp.where(
                        frame >= BASE_WIN, gone.astype(jnp.float32), 0.0
                    )
                delta = (value - running * inv_ref[frame]).astype(jnp.bfloat16)
                delta_ref[frame, :, span] = delta
                delta32[lane // LANES, pl.ds(frame * rows, rows), :] = delta.astype(
                    jnp.float32
                )
            return (running, *history)

        lax.fori_loop(0, devices, block_step, (zero,) * taps)

    total = prev_ref[...]
    for row in range(rows):
        picked = jnp.concatenate(
            [
                delta32[tile, pl.ds(row, frames, stride=rows), :].astype(jnp.bfloat16)
                for tile in range(width // LANES)
            ],
            axis=1,
        )
        total = total + lax.dot_general(
            dense_ref[row],
            picked,
            (((1,), (1,)), ((), ())),
            preferred_element_type=jnp.float32,
        )
    roi_here = total.shape[0] // owners
    if last:
        partial[...] = total.reshape(owners, roi_here, frames)
        for k in range(owners):
            part_refs[k][...] = partial[position ^ k]
    else:
        part_refs[0][...] = total


def run_chunk(ids, inverse, coeffs, dense, prev, blocks, places, owners, last):
    devices = len(blocks)
    step = blocks[0].shape[0]
    _, rows, width = coeffs.shape
    frames = devices * step
    rois = dense.shape[1]
    vmem = pl.BlockSpec(memory_space=pltpu.VMEM)
    smem = pl.BlockSpec(memory_space=pltpu.SMEM)
    held = frames if frames > BASE_WIN else 1
    parts = owners if last else 1
    return pl.pallas_call(
        functools.partial(chunk_kernel, places=tuple(places), owners=owners, last=last),
        out_shape=[jax.ShapeDtypeStruct((frames, rows, width), jnp.bfloat16)]
        + [jax.ShapeDtypeStruct((rois // parts, frames), jnp.float32)] * parts,
        in_specs=[smem, smem] + [vmem] * (3 + devices),
        out_specs=[vmem] * (1 + parts),
        scratch_shapes=[
            pltpu.VMEM((frames, rows, width), jnp.bfloat16),
            pltpu.VMEM((held, rows, width), jnp.bfloat16),
            pltpu.VMEM((width // LANES, (frames + 1) * rows, LANES), jnp.float32),
            pltpu.VMEM((owners, rois // owners, frames), jnp.float32),
        ],
        compiler_params=pltpu.CompilerParams(vmem_limit_bytes=24 * 1024 * 1024),
        cost_estimate=pl.CostEstimate(
            flops=2 * frames * rows * width * rois,
            bytes_accessed=4 * frames * rows * width,
            transcendentals=0,
        ),
    )(ids, inverse, coeffs, dense, prev, *blocks)


REACH = 8


def filtered_at(now, history, weights):
    total = weights[0] * now
    for tap in range(1, len(weights)):
        total = total + weights[tap] * history[tap - 1]
    return total.astype(jnp.bfloat16).astype(jnp.float32)


def tap_weights(coeff_ref, tile):
    span = slice(tile * LANES, (tile + 1) * LANES)
    return [coeff_ref[tap, :, span].astype(jnp.float32) for tap in range(coeff_ref.shape[0])]


def frame_rows(frame, rows):
    return pl.ds(pl.multiple_of(frame * rows, rows), rows)


def filter_rows(pixels, filtered, coeff_ref, frames, step):
    taps, rows, _ = coeff_ref.shape
    for tile in range(pixels.shape[0]):
        weights = tap_weights(coeff_ref, tile)

        def block_step(index, history):
            history = list(history)
            for offset in range(step):
                at = frame_rows(index * step + offset, rows)
                now = pixels[tile, at, :]
                filtered[tile, at, :] = filtered_at(now, history, weights)
                history = [now] + history[:-1]
            return tuple(history)

        zero = jnp.zeros((rows, LANES), jnp.float32)
        lax.fori_loop(0, frames // step, block_step, (zero,) * (taps - 1))


def project(filtered, dense_ref, first, frames):
    rows, tiles = dense_ref.shape[0], filtered.shape[0]
    joined = max(1, 256 // (tiles * LANES))
    total = 0.0
    for row in range(0, rows, joined):
        several = range(row, min(row + joined, rows))
        picked = [
            filtered[tile, pl.ds(first * rows + one, frames, stride=rows), :].astype(jnp.bfloat16)
            for one in several
            for tile in range(tiles)
        ]
        total = total + lax.dot_general(
            jnp.concatenate([dense_ref[one] for one in several], axis=1),
            jnp.concatenate(picked, axis=1),
            (((1,), (1,)), ((), ())),
            preferred_element_type=jnp.float32,
        )
    return total


def fill(pixels, blocks, places, here, step, rows):
    for block, (k, lane) in zip(blocks, places):
        start = pl.multiple_of((here ^ k) * (step * rows), step * rows)
        for tile in range(pixels.shape[0]):
            first = lane + tile * LANES
            pixels[tile, pl.ds(start, step * rows), :] = block[
                :, first : first + LANES
            ].astype(jnp.float32)


def late_frames(here, late, step):
    return (here ^ late[-1]) // len(late) * (len(late) * step), len(late) * step + REACH


def minus_mean(total):
    frames = total.shape[1]
    earlier = lax.broadcasted_iota(jnp.int32, (frames, frames), 0)
    later = lax.broadcasted_iota(jnp.int32, (frames, frames), 1)
    upto = jnp.where(earlier <= later, 1.0, 0.0).astype(jnp.bfloat16)
    high = total.astype(jnp.bfloat16)
    rest = total - high.astype(jnp.float32)
    middle = rest.astype(jnp.bfloat16)
    low = (rest - middle.astype(jnp.float32)).astype(jnp.bfloat16)
    terms = jnp.concatenate([low, middle, high], axis=0)
    sums = jnp.dot(terms, upto, preferred_element_type=jnp.float32)
    height = total.shape[0]
    running = sums[:height] + sums[height : 2 * height] + sums[2 * height :]
    frame_ids = lax.broadcasted_iota(jnp.int32, total.shape, 1)
    return total - running / jnp.minimum(frame_ids + 1, BASE_WIN).astype(jnp.float32)


def early_kernel(coeff_ref, dense_ref, *rest, places, step, frames, late):
    blocks = rest[: len(places)]
    pixels, filtered, total_ref = rest[len(places) :]
    rows = coeff_ref.shape[1]
    here = lax.axis_index("tm")
    first, length = late_frames(here, late, step)
    at = pl.ds(pl.multiple_of(first * rows, step * rows), length * rows)
    zeros = jnp.zeros((length * rows, LANES), jnp.float32)
    for tile in range(pixels.shape[0]):
        pixels[tile, at, :] = zeros
    fill(pixels, blocks, [(k, 0) for k in places], here, step, rows)
    filter_rows(pixels, filtered, coeff_ref, frames, step)
    for tile in range(pixels.shape[0]):
        filtered[tile, at, :] = zeros
    total_ref[...] = project(filtered, dense_ref, 0, frames)


def late_kernel(coeff_ref, dense_ref, total_ref, pixels, *rest, late, first_tile, last):
    blocks = rest[: len(late)]
    filtered, *outs, held, strip, partial = rest[len(late) :]
    here, position = lax.axis_index("tm"), lax.axis_index("roi")
    taps, rows, width = coeff_ref.shape
    step = blocks[0].shape[0] // rows
    frames = total_ref.shape[1]
    first, length = late_frames(here, late, step)
    for tile in range(width // LANES):
        own = pixels.at[first_tile + tile]
        for block, k in zip(blocks, late):
            start = pl.multiple_of(((here ^ k) * step - first) * rows, step * rows)
            held[pl.ds(start, step * rows), :] = block[
                :, tile * LANES : (tile + 1) * LANES
            ].astype(jnp.float32)
        after = pl.multiple_of((first + length - REACH) * rows, step * rows)
        held[pl.ds((length - REACH) * rows, REACH * rows), :] = own[pl.ds(after, REACH * rows), :]
        weights = tap_weights(coeff_ref, tile)
        history = []
        for tap in range(1, taps):
            earlier = own[frame_rows(jnp.maximum(first - tap, 0), rows), :]
            history.append(jnp.where(first > 0, earlier, 0.0))

        def block_step(index, history):
            history = list(history)
            for offset in range(REACH):
                at = frame_rows(index * REACH + offset, rows)
                now = held[at, :]
                filtered[tile, at, :] = filtered_at(now, history, weights)
                history = [now] + history[:-1]
            return tuple(history)

        lax.fori_loop(0, length // REACH, block_step, tuple(history))
    strip[...] = jnp.zeros(strip.shape, jnp.float32)
    strip[:, :length] = project(filtered, dense_ref, 0, length)
    frame_ids = lax.broadcasted_iota(jnp.int32, strip.shape, 1)
    found = jnp.where(frame_ids < frames - first, strip[...], 0.0)
    total = total_ref[...] + pltpu.roll(found, first, 1)
    if last:
        partial[...] = minus_mean(total).reshape(partial.shape)
        for k, out in enumerate(outs):
            out[...] = partial[position ^ k]
    else:
        outs[0][...] = total


def delta_kernel(*rest, late, step):
    *pieces, filtered, out_ref, inv_ref, packed, sems = rest
    tiles, frames, rows, _ = packed.shape
    first, length = late_frames(lax.axis_index("tm"), late, step)
    end = jnp.minimum(first + length, frames)
    counts = lax.broadcasted_iota(jnp.int32, (frames, LANES), 0) + 1
    inv_ref[...] = 1.0 / jnp.minimum(counts, BASE_WIN).astype(jnp.float32)
    places = [(piece, tile) for piece in pieces[::-1] for tile in range(piece.shape[0])]
    copies = []
    for tile in range(0, tiles, 2):
        several = range(tile, min(tile + 2, tiles))

        def subtract_mean(source, low, high, running):
            def block_step(index, running):
                running = list(running)
                for offset in range(REACH):
                    frame = index * REACH + offset
                    for turn, one in enumerate(several):
                        value = source(one, frame)
                        running[turn] = running[turn] + value
                        packed[one, frame] = (value - running[turn] * inv_ref[pl.ds(frame, 1), :]).astype(
                            jnp.bfloat16
                        )
                return tuple(running)

            return lax.fori_loop(low // REACH, high // REACH, block_step, running)

        def early(one, frame):
            return filtered[one, frame_rows(frame, rows), :]

        def middle(one, frame):
            piece, its_tile = places[one]
            return piece[its_tile, frame_rows(frame - first, rows), :]

        zero = jnp.zeros((rows, LANES), jnp.float32)
        running = subtract_mean(early, 0, first, (zero,) * len(several))
        running = subtract_mean(middle, first, end, running)
        subtract_mean(early, end, frames, running)
        for one in several:
            place = out_ref.at[:, :, pl.ds(one * LANES, LANES)]
            copies.append(pltpu.make_async_copy(packed.at[one], place, sems.at[one]))
            copies[-1].start()
    for copy in copies:
        copy.wait()


VMEM = pl.BlockSpec(memory_space=pltpu.VMEM)
SMEM = pl.BlockSpec(memory_space=pltpu.SMEM)
ANYWHERE = pl.BlockSpec(memory_space=pl.ANY)


def options(mib, work):
    return dict(
        compiler_params=pltpu.CompilerParams(vmem_limit_bytes=mib * 1024 * 1024),
        cost_estimate=pl.CostEstimate(flops=16 * work, bytes_accessed=4 * work, transcendentals=0),
    )


def run_early(coeffs, dense, blocks, places, frames, late):
    _, rows, width = coeffs.shape
    step = blocks[0].shape[0] // rows
    held = jax.ShapeDtypeStruct((width // LANES, (frames + 2 * REACH) * rows, LANES), jnp.float32)
    return pl.pallas_call(
        functools.partial(
            early_kernel, places=tuple(places), step=step, frames=frames, late=tuple(late)
        ),
        out_shape=[held, held, jax.ShapeDtypeStruct((dense.shape[1], frames), jnp.float32)],
        in_specs=[VMEM] * (2 + len(blocks)),
        out_specs=[VMEM] * 3,
        **options(4, frames * rows * width),
    )(coeffs, dense, *blocks)


def run_late(coeffs, dense, total, pixels, late, owners, first_tile, last):
    _, rows, width = coeffs.shape
    rois, frames = total.shape
    height = sum(block.shape[0] for block in late.values()) + (REACH + 1) * rows
    parts = owners if last else 1
    part = jax.ShapeDtypeStruct((rois // parts, frames), jnp.float32)
    return pl.pallas_call(
        functools.partial(late_kernel, late=tuple(late), first_tile=first_tile, last=last),
        out_shape=[jax.ShapeDtypeStruct((width // LANES, height, LANES), jnp.float32)]
        + [part] * parts,
        in_specs=[VMEM] * (4 + len(late)),
        out_specs=[VMEM] * (1 + parts),
        scratch_shapes=[
            pltpu.VMEM((height, LANES), jnp.float32),
            pltpu.VMEM((rois, frames), jnp.float32),
            pltpu.VMEM((owners, rois // owners, frames), jnp.float32),
        ],
        **options(4, frames * rows * width),
    )(coeffs, dense, total, pixels, *late.values())


def run_delta(filtered, pieces, late, rows, step):
    tiles, frames = filtered.shape[0], filtered.shape[1] // rows - 2 * REACH
    return pl.pallas_call(
        functools.partial(delta_kernel, late=tuple(late), step=step),
        out_shape=jax.ShapeDtypeStruct((frames, rows, tiles * LANES), jnp.bfloat16),
        in_specs=[VMEM] * (1 + len(pieces)),
        out_specs=ANYWHERE,
        scratch_shapes=[
            pltpu.VMEM((frames, LANES), jnp.float32),
            pltpu.VMEM((tiles, frames, rows, LANES), jnp.bfloat16),
            pltpu.SemaphoreType.DMA((tiles,)),
        ],
        **options(4, frames * rows * tiles * LANES),
    )(*pieces[::-1], filtered)


def swaps(count, k):
    return [(i, i ^ k) for i in range(count)]


def plain_plan(movie, coeffs, dense_of, ids, inverse, here, position, devices, owners):
    step, _, slab_width = movie.shape
    rows = coeffs.shape[1]
    frames = devices * step
    middle = slab_width // LANES // 2 * LANES
    cuts = [0, middle, slab_width]
    near = list(range(devices // 2 - 1, 0, -1))
    far = list(range(devices - 1, devices // 2 - 1, -1))
    split = far[len(far) // 2 :]
    opening = [(k, 0, slab_width) for k in far[: len(far) // 2]]
    beside = [(k, 0, slab_width) for k in near]
    first = [(k, 0, middle) for k in split]
    second = [(k, middle, slab_width) for k in split]
    ties = dict(zip(first + second, beside[::-1][: len(first) - 1] + opening + first))

    def rows_of(source, k, low, high):
        return lax.dynamic_slice(source, (0, (here ^ k) * rows, low), (step, rows, high - low))

    blocks = [rows_of(movie, *item) for item in opening]
    rest, *blocks = lax.optimization_barrier((movie, *blocks))
    arrived = {}
    for item in opening + beside + first + second:
        block = blocks.pop(0) if blocks else rows_of(rest, *item)
        if item in ties:
            block, arrived[ties[item]] = lax.optimization_barrier((block, arrived[ties[item]]))
        arrived[item] = lax.ppermute(block, "tm", swaps(devices, item[0]))
    arrived[0, 0, slab_width] = rows_of(rest, 0, 0, slab_width)
    chunks = []
    for low, high in zip(cuts[:-1], cuts[1:]):
        chunks.append(
            [
                (block, (k, low - start))
                for (k, start, end), block in arrived.items()
                if start <= low and high <= end
            ]
        )

    dense = dense_of()
    prev = jnp.zeros((dense.shape[1], frames), jnp.float32)
    deltas = []
    for low, high, received in zip(cuts[:-1], cuts[1:], chunks):
        delta, *parts = run_chunk(
            ids,
            inverse,
            coeffs[:, :, low:high],
            dense[:, :, low:high],
            prev,
            [block for block, _ in received],
            [place for _, place in received],
            owners,
            high == slab_width,
        )
        deltas.append(delta)
        prev = parts[0]
    traces = parts[0]
    for k in range(1, owners):
        traces = traces + lax.ppermute(parts[k], "roi", swaps(owners, k))
    return jnp.concatenate(deltas, axis=2), traces


def local(movie, coeffs, footprint_w, roi_blocks, roi_len):
    devices = lax.axis_size("tm")
    owners = lax.axis_size("roi")
    here = lax.axis_index("tm")
    position = lax.axis_index("roi")
    step, _, slab_width = movie.shape
    rows = coeffs.shape[1]
    frames = devices * step
    slot_count = roi_blocks.shape[1]

    live = jnp.arange(slot_count, dtype=jnp.int32)[None, :] < roi_len[:, None]
    live = live & (roi_blocks // rows == position)
    hit = live[:, :, None] & (
        (roi_blocks % rows)[:, :, None] == jnp.arange(rows, dtype=jnp.int32)
    )

    def dense_of():
        gathered = lax.all_gather(footprint_w, "roi", axis=0, tiled=True)
        return sum(
            jnp.where(hit[:, m, :].T[:, :, None], gathered[None, :, m, :], 0)
            for m in range(slot_count)
        ).astype(jnp.bfloat16)

    counts = jnp.minimum(jnp.arange(frames, dtype=jnp.int32) + 1, BASE_WIN)
    inverse = 1.0 / counts.astype(jnp.float32)
    middle = slab_width - LANES
    ids = jnp.stack([here, position]).astype(jnp.int32)
    if frames > BASE_WIN or devices % 4 or middle == 0:
        return plain_plan(
            movie, coeffs, dense_of, ids, inverse, here, position, devices, owners
        )

    far = list(range(devices - 1, devices // 2 - 1, -1))
    near = list(range(1, devices // 2))
    early, late = far[: len(far) // 2], far[len(far) // 2 :]

    def rows_of(source, k, low=0, high=slab_width):
        block = lax.dynamic_slice(
            source, (0, (here ^ k) * rows, low), (step, rows, high - low)
        )
        return block.reshape(step * rows, high - low)

    def send(block, k, *after):
        if after:
            block, *_ = lax.optimization_barrier((block, *after))
        return lax.ppermute(block, "tm", swaps(devices, k))

    opening = rows_of(movie, early[0])
    rest, opening = lax.optimization_barrier((movie, opening))
    whole = {early[0]: send(opening, early[0])}
    whole |= {k: send(rows_of(rest, k), k) for k in early[1:]}
    whole |= {k: send(rows_of(rest, k), k) for k in near}
    ties = [whole[near[0]]] + [whole[k] for k in early]
    low = {k: send(rows_of(rest, k, 0, middle), k, tie) for k, tie in zip(late, ties)}
    ties = ties[len(late) :] + list(low.values())
    high = {k: send(rows_of(rest, k, middle), k, tie) for k, tie in zip(late, ties)}
    whole[0] = rows_of(rest, 0)
    dense = dense_of()

    pixels, filtered, total = run_early(
        coeffs, dense, list(whole.values()), list(whole), frames, late
    )
    lower, total = run_late(
        coeffs[:, :, :middle],
        dense[:, :, :middle],
        total,
        pixels,
        low,
        owners,
        0,
        False,
    )
    pixels, filtered, lower, total = lax.optimization_barrier(
        (pixels, filtered, lower, total)
    )
    upper, *parts = run_late(
        coeffs[:, :, middle:],
        dense[:, :, middle:],
        total,
        pixels,
        high,
        owners,
        middle // LANES,
        True,
    )
    traces = parts[0]
    for k in range(1, owners):
        traces = traces + lax.ppermute(parts[k], "roi", swaps(owners, k))
    delta = run_delta(filtered, [lower, upper], late, rows, step)
    return delta, traces


def solution(mesh):
    placed = (
        P("tm", None, "roi"),
        P(None, "tm", "roi"),
        P(("tm", "roi"), None, None),
        P("tm", None),
        P("tm"),
    )
    return jax.shard_map(
        local,
        mesh=mesh,
        in_specs=placed,
        out_specs=(P(None, "tm", "roi"), P(("tm", "roi"), None)),
        check_vma=False,
    )
```
